32 devices in a mesh: dp: 2 (over y), row: 4 (over z), col: 4 (over x, core).
Axes of the slice: x: 2, y: 2, z: 4, core: 2. Of those that a mesh axis runs over, the one named last changes fastest.
Arguments:
- image_tokens: bfloat16 [8192, 1536], P(('dp', 'col'), 'row'), may hold values from -6 to 6
- text_tokens: bfloat16 [1232, 1536], P(('dp', 'col'), 'row'), may hold values from -6 to 6
- condition: bfloat16 [8, 1536], P('dp', 'col'), may hold values from -6 to 6
- ada_w: bfloat16 [2, 1536, 6, 1536], P(None, 'col', None, 'row'), may hold values from -0.15625 to 0.15625
- ada_b: bfloat16 [2, 6, 1536], P(None, None, 'row'), may hold values from -3 to 3
- qkv_w: bfloat16 [2, 1536, 3, 1536], P(None, 'row', None, 'col'), may hold values from -0.15625 to 0.15625
- qkv_b: bfloat16 [2, 2, 1536], P(None, None, 'col'), may hold values from -3 to 3
- out_w: bfloat16 [2, 1536, 1536], P(None, 'col', 'row'), may hold values from -0.4375 to 0.4375
- out_b: bfloat16 [2, 1536], P(None, 'row'), may hold values from -3 to 3
- up_w: bfloat16 [2, 1536, 6144], P(None, 'row', 'col'), may hold values from -0.15625 to 0.15625
- up_b: bfloat16 [2, 6144], P(None, 'col'), may hold values from -3 to 3
- down_w: bfloat16 [2, 6144, 1536], P(None, 'col', 'row'), may hold values from -0.078125 to 0.078125
- down_b: bfloat16 [2, 1536], P(None, 'row'), may hold values from -3 to 3
- image_cot: bfloat16 [8192, 1536], P(('dp', 'col'), 'row'), may hold values from -6 to 6
- text_cot: bfloat16 [1232, 1536], P(('dp', 'col'), 'row'), may hold values from -6 to 6
Outputs:
- image_out: bfloat16 [8192, 1536], P(('dp', 'col'), 'row')
- text_out: bfloat16 [1232, 1536], P(('dp', 'col'), 'row')
- image_grad: float32 [8192, 1536], P(('dp', 'col'), 'row')
- text_grad: float32 [1232, 1536], P(('dp', 'col'), 'row')
- condition_grad: float32 [8, 1536], P('dp', 'col')
- grad_ada_w: float32 [2, 1536, 6, 1536], P(None, 'col', None, 'row')
- grad_ada_b: float32 [2, 6, 1536], P(None, None, 'row')
- grad_qkv_w: float32 [2, 1536, 3, 1536], P(None, 'row', None, 'col')
- grad_qkv_b: float32 [2, 2, 1536], P(None, None, 'col')
- grad_out_w: float32 [2, 1536, 1536], P(None, 'col', 'row')
- grad_out_b: float32 [2, 1536], P(None, 'row')
- grad_up_w: float32 [2, 1536, 6144], P(None, 'row', 'col')
- grad_up_b: float32 [2, 6144], P(None, 'col')
- grad_down_w: float32 [2, 6144, 1536], P(None, 'col', 'row')
- grad_down_b: float32 [2, 1536], P(None, 'row')
The draws below stay inside these ranges and needn't reach their ends.
All inputs are finite; a program needn't handle non-finite values.
Results may differ from the reference program's by a relative error of at most 0.015.
The reference program's roundings to bfloat16 on the way count: a program that leaves them out, or rounds other values in their place, can miss the bound.
Values may be sent and summed in bfloat16 or wider, within the bound.
A program may use at most 320 MiB of HBM per device.

```python
import jax
import jax.numpy as jnp
from jax import lax

D = 1536
HEADS = 24
HEAD = 64
FF = 6144
IMG = 1024
TXT = 154
SEQS = 8


def block_levels(key, dims, cuts, low, top_value):
    factor_of = 1.0
    for dim, blocks in cuts:
        steps = jax.random.uniform(jax.random.fold_in(jax.random.fold_in(key, 6), dim), (blocks,), jnp.float32, low / len(cuts), top_value / len(cuts))
        factor_of = factor_of * jnp.repeat(jnp.exp(steps), dims[dim] // blocks).reshape((-1,) + (1,) * (len(dims) - 1 - dim))
    return factor_of


def noise(stream_key, dims, width, most, split=(), dtype=jnp.bfloat16):
    factor_of = block_levels(stream_key, dims, split, -0.22, 0.18) if split else 1.0
    result = jax.random.normal(stream_key, dims, jnp.float32) * width * factor_of
    return jnp.minimum(jnp.maximum(result, -most), most).astype(dtype)


def setup_inputs(seed: int = 0) -> dict:
    streams_of = jax.random.split(jax.random.key(seed), 16)
    return {
        "image_tokens": noise(streams_of[0], (SEQS * IMG, D), 1.0, 6.0, ((0, 8), (1, 4))),
        "text_tokens": noise(streams_of[1], (SEQS * TXT, D), 1.0, 6.0, ((0, 8), (1, 4))),
        "condition": noise(streams_of[2], (SEQS, D), 1.0, 6.0, ((0, 2), (1, 4))),
        "ada_w": noise(streams_of[3], (2, D, 6, D), D ** -0.5, 0.15625, ((1, 4), (3, 4))),
        "ada_b": noise(streams_of[4], (2, 6, D), 0.5, 3.0, ((2, 4),)),
        "qkv_w": noise(streams_of[5], (2, D, 3, D), D ** -0.5, 0.15625, ((1, 4), (3, 4))),
        "qkv_b": noise(streams_of[6], (2, 2, D), 0.5, 3.0, ((2, 4),)),
        "out_w": noise(streams_of[7], (2, D, D), (D // 8) ** -0.5, 0.4375, ((1, 4), (2, 4))),
        "out_b": noise(streams_of[8], (2, D), 0.5, 3.0, ((1, 4),)),
        "up_w": noise(streams_of[9], (2, D, FF), D ** -0.5, 0.15625, ((1, 4), (2, 4))),
        "up_b": noise(streams_of[10], (2, FF), 0.5, 3.0, ((1, 4),)),
        "down_w": noise(streams_of[11], (2, FF, D), FF ** -0.5, 0.078125, ((1, 4), (2, 4))),
        "down_b": noise(streams_of[12], (2, D), 0.5, 3.0, ((1, 4),)),
        "image_cot": noise(streams_of[13], (SEQS * IMG, D), 1.0, 6.0, ((0, 8), (1, 4))),
        "text_cot": noise(streams_of[14], (SEQS * TXT, D), 1.0, 6.0, ((0, 8), (1, 4))),
    }


@jax.custom_vjp
def low(v):
    return lax.optimization_barrier(v.astype(jnp.bfloat16)).astype(jnp.float32)

@jax.custom_vjp
def low_back(v):
    return v

def low_keep(v):
    return (low(v), None)

def low_pass(kept, grad):
    return (grad,)

def back_keep(v):
    return (v, None)

def back_low(kept, grad):
    return (low(grad),)
low.defvjp(low_keep, low_pass)
low_back.defvjp(back_keep, back_low)

def matmul(left, right):
    return jnp.dot(left, right, precision=lax.Precision.HIGHEST)

def layer_norm(values):
    mean = lax.optimization_barrier(jnp.mean(values, axis=-1, keepdims=True))
    spread = lax.optimization_barrier(jnp.mean(values * values, axis=-1, keepdims=True)) - mean * mean
    return (values - mean) * lax.rsqrt(spread + 1e-06)

def stream_front(tokens, modul, weight, bias):
    mixed = low(layer_norm(tokens) * (1.0 + modul[1]) + modul[0])
    qkv = matmul(mixed, weight.reshape(D, 3 * D)).reshape(-1, 3, D)
    full_bias = jnp.stack([bias[0], jnp.zeros_like(bias[0]), bias[1]])
    return low_back(low(qkv + full_bias))

def stream_back(tokens, attn, modul, out_w, out_b, up_w, up_b, down_w, down_b):
    attn = low_back(low(attn))
    proj = low_back(matmul(attn, out_w) + out_b)
    resid = tokens + modul[2] * proj
    mixed = low(layer_norm(resid) * (1.0 + modul[4]) + modul[3])
    pre = low_back(matmul(mixed, up_w) + up_b)
    hidden = low(jax.nn.gelu(pre, approximate=True))
    branch = low_back(matmul(hidden, down_w) + down_b)
    return resid + modul[5] * branch

def one_sequence(params, image, text, cond):
    ada_w, ada_b, qkv_w, qkv_b, out_w, out_b, up_w, up_b, down_w, down_b = params
    lowered = low(jax.nn.silu(cond))
    mods = []
    for stream in range(2):
        raw = matmul(lowered[None, :], ada_w[stream].reshape(D, 6 * D)).reshape(6, D)
        mods.append(low_back(raw + ada_b[stream]))
    qkv_image = stream_front(image, mods[0], qkv_w[0], qkv_b[0])
    qkv_text = stream_front(text, mods[1], qkv_w[1], qkv_b[1])
    qkv = jnp.concatenate([qkv_image, qkv_text], axis=0)
    length = IMG + TXT
    query = qkv[:, 0].reshape(length, HEADS, HEAD)
    keys = qkv[:, 1].reshape(length, HEADS, HEAD)
    values = qkv[:, 2].reshape(length, HEADS, HEAD)
    scores = low_back(jnp.einsum('qhd,khd->hqk', query, keys, precision=lax.Precision.HIGHEST) * HEAD ** (-0.5))
    prob = low(jax.nn.softmax(scores, axis=-1))
    attn = jnp.einsum('hqk,khd->qhd', prob, values, precision=lax.Precision.HIGHEST).reshape(length, D)
    out_image = stream_back(image, attn[:IMG], mods[0], out_w[0], out_b[0], up_w[0], up_b[0], down_w[0], down_b[0])
    out_text = stream_back(text, attn[IMG:], mods[1], out_w[1], out_b[1], up_w[1], up_b[1], down_w[1], down_b[1])
    return (out_image, out_text)

def reference(image_tokens, text_tokens, condition, ada_w, ada_b, qkv_w, qkv_b, out_w, out_b, up_w, up_b, down_w, down_b, image_cot, text_cot):
    params = tuple((item.astype(jnp.float32) for item in (ada_w, ada_b, qkv_w, qkv_b, out_w, out_b, up_w, up_b, down_w, down_b)))
    images = image_tokens.astype(jnp.float32).reshape(SEQS, IMG, D)
    texts = text_tokens.astype(jnp.float32).reshape(SEQS, TXT, D)
    conds = condition.astype(jnp.float32)
    image_cots = image_cot.astype(jnp.float32).reshape(SEQS, IMG, D)
    text_cots = text_cot.astype(jnp.float32).reshape(SEQS, TXT, D)

    def step(total, item):
        image, text, cond, cot_image, cot_text = item
        outs, pull = jax.vjp(one_sequence, params, image, text, cond)
        grads = pull((cot_image, cot_text))
        total = jax.tree.map(jnp.add, total, grads[0])
        return (total, (outs[0], outs[1], grads[1], grads[2], grads[3]))
    zero = jax.tree.map(jnp.zeros_like, params)
    total, results = lax.scan(step, zero, (images, texts, conds, image_cots, text_cots))
    out_image, out_text, grad_image, grad_text, grad_cond = results
    return (out_image.reshape(SEQS * IMG, D).astype(jnp.bfloat16), out_text.reshape(SEQS * TXT, D).astype(jnp.bfloat16), grad_image.reshape(SEQS * IMG, D), grad_text.reshape(SEQS * TXT, D), grad_cond, total[0], total[1], total[2], total[3], total[4], total[5], total[6], total[7], total[8], total[9])
```

```python
import functools

import jax
import jax.numpy as jnp
from jax import lax
from jax.experimental import pallas as pl
from jax.experimental.pallas import tpu as pltpu
from jax.sharding import PartitionSpec as P

D = 1536
HEAD = 64
IMG = 1024
TXT = 154
PAD = 160
SCALE = HEAD**-0.5
EPSILON = 1e-06
BF = jnp.bfloat16
F32 = jnp.float32


def product(left, right):
    return jnp.dot(left, right, preferred_element_type=F32)


def product_left(left, right):
    return lax.dot_general(left, right, (((0,), (0,)), ((), ())), preferred_element_type=F32)


def product_right(left, right):
    return lax.dot_general(left, right, (((1,), (1,)), ((), ())), preferred_element_type=F32)


def gelu_value(values):
    return jax.nn.gelu(values, approximate=True)


def gelu_slope(values, grad):
    return jax.vjp(gelu_value, values)[1](grad)[0]


def silu_slope(values, grad):
    return jax.vjp(jax.nn.silu, values)[1](grad)[0]


def gather(values, axis_name, axis=0):
    return lax.all_gather(values, axis_name, axis=axis, tiled=True)


def shifted(values, count, step):
    return lax.ppermute(values, "dp", [(i, (i + step) % count) for i in range(count)])


def partner(values, count):
    return lax.ppermute(values, "dp", [(i, i ^ 1) for i in range(count)])


def in_order(mine, other, parity, axis):
    first = jnp.where(parity == 0, mine, other)
    second = jnp.where(parity == 0, other, mine)
    return jnp.stack([first, second], axis=axis)


def sum_over_dp(values, count):
    total = values.astype(F32)
    for step in range(1, count):
        total = total + shifted(values, count, step).astype(F32)
    return total


def join_over_dp(values, count, parity):
    mine = values.astype(F32)
    other = shifted(values, count, 1).astype(F32)
    for step in range(2, count):
        moved = shifted(values, count, step).astype(F32)
        if step % 2:
            other = other + moved
        else:
            mine = mine + moved
    joined = in_order(mine, other, parity, 0)
    return joined.reshape((-1,) + values.shape[1:])


def gather_block(block, count, parity):
    half = lax.dynamic_index_in_dim(block.reshape(2, -1, block.shape[1]), parity, 0, keepdims=False)
    mine = lax.all_gather(half, "row")
    both = in_order(mine, partner(mine, count), parity, 1)
    return both.reshape(mine.shape[0], -1, mine.shape[2])


def after(value, *others):
    return lax.optimization_barrier((value, others))[0]


def norm_local(values):
    mean = jnp.mean(values, axis=1, keepdims=True)
    square = jnp.mean(values * values, axis=1, keepdims=True)
    inverse = lax.rsqrt(square - mean * mean + EPSILON)
    return (values - mean) * inverse, inverse


def norm_local_back(grad, normed, inverse):
    total = jnp.mean(grad, axis=1, keepdims=True)
    cross = jnp.mean(grad * normed, axis=1, keepdims=True)
    return inverse * (grad - total - normed * cross)


def row_stats(first, second):
    pair = jnp.stack([jnp.sum(first, axis=1), jnp.sum(second, axis=1)])
    return jnp.pad(pair, ((0, 6), (0, 0)))


def row_means(stats):
    totals = jnp.sum(stats.reshape(4, 8, -1)[:, :2], axis=0) / D
    return totals[0][:, None], totals[1][:, None]


def norm_row(values, stats):
    mean, square = row_means(stats)
    inverse = lax.rsqrt(square - mean * mean + EPSILON)
    return (values - mean) * inverse, inverse


def norm_row_back(grad, normed, inverse, stats):
    total, cross = row_means(stats)
    return inverse * (grad - total - normed * cross)


def side(values, rows):
    width = values.shape[1]
    return values.reshape(rows, -1, width).transpose(1, 0, 2).reshape(-1, rows * width)


def stack(values, rows):
    count = values.shape[0]
    return values.reshape(count, rows, -1).transpose(1, 0, 2).reshape(rows * count, -1)


LOG2 = 1.4426950408889634


def dot_nt(left, right):
    return lax.dot_general(left, right, (((1,), (1,)), ((), ())), preferred_element_type=F32)


def dot_tn(left, right):
    return lax.dot_general(left, right, (((0,), (0,)), ((), ())), preferred_element_type=F32)


def head_mask(values, head):
    lane = lax.broadcasted_iota(jnp.int32, values.shape, 1)
    return jnp.where((lane >= head * HEAD) & (lane < (head + 1) * HEAD), values, 0)


def attend_kernel(qi, ki, vi, qt, kt, vt, oi, ot, li, lt, kim, vim, ktm, vtm):
    for h in range(2):
        kim[h] = head_mask(ki[...], h)
        vim[h] = head_mask(vi[...], h)
        ktm[h] = head_mask(kt[...], h)
        vtm[h] = head_mask(vt[...], h)

    def block(query):
        total = None
        rows = []
        for h in range(2):
            si = dot_nt(query, kim[h])
            st = dot_nt(query, ktm[h])
            lane = lax.broadcasted_iota(jnp.int32, st.shape, 1)
            st = jnp.where(lane < TXT, st, -1e30)
            peak = jnp.maximum(
                jnp.max(si, axis=1, keepdims=True), jnp.max(st, axis=1, keepdims=True)
            )
            ei = jnp.exp2((si - peak) * (SCALE * LOG2))
            et = jnp.exp2((st - peak) * (SCALE * LOG2))
            norm = jnp.sum(ei, axis=1, keepdims=True) + jnp.sum(et, axis=1, keepdims=True)
            part = product(ei.astype(BF), vim[h]) + product(et.astype(BF), vtm[h])
            part = part / norm
            total = part if total is None else total + part
            rows.append(peak * (SCALE * LOG2) + jnp.log2(norm))
        lane = lax.broadcasted_iota(jnp.int32, total.shape, 1)
        stats = jnp.where(lane == 0, rows[0], jnp.where(lane == 1, rows[1], 0.0))
        return total.astype(BF), jnp.transpose(stats)[:8]

    for b in range(IMG // 256):
        at = pl.ds(b * 256, 256)
        oi[at, :], li[0, :, at] = block(qi[at, :])
    ot[...], lt[0] = block(qt[...])


def attend(qkv_i, qkv_t):
    width = qkv_i.shape[1] // 3
    pairs = width // 128

    def part(rows, which):
        return pl.BlockSpec((rows, 128), lambda j: (0, which * pairs + j))

    return pl.pallas_call(
        attend_kernel,
        grid=(pairs,),
        in_specs=[part(n, w) for n in (IMG, PAD) for w in range(3)],
        out_specs=[
            part(IMG, 0),
            part(PAD, 0),
            pl.BlockSpec((1, 8, IMG), lambda j: (j, 0, 0)),
            pl.BlockSpec((1, 8, PAD), lambda j: (j, 0, 0)),
        ],
        out_shape=[
            jax.ShapeDtypeStruct((IMG, width), BF),
            jax.ShapeDtypeStruct((PAD, width), BF),
            jax.ShapeDtypeStruct((pairs, 8, IMG), F32),
            jax.ShapeDtypeStruct((pairs, 8, PAD), F32),
        ],
        scratch_shapes=[pltpu.VMEM((2, n, 128), BF) for n in (IMG, IMG, PAD, PAD)],
        compiler_params=pltpu.CompilerParams(vmem_limit_bytes=56 * 1024 * 1024),
        cost_estimate=cost(19),
        name="attend",
    )(qkv_i, qkv_i, qkv_i, qkv_t, qkv_t, qkv_t)


def attend_back_kernel(
    qi, ki, vi, qt, kt, vt, oi, ot, gi, gt, li, lt, dqi, dki, dvi, dqt, dkt, dvt, aki, avi, akt, avt
):
    for acc in (aki, avi, akt, avt):
        acc[...] = jnp.zeros_like(acc)
    lane8 = lax.broadcasted_iota(jnp.int32, (8, 128), 1) // HEAD
    row8 = lax.broadcasted_iota(jnp.int32, (8, 128), 0)
    pick = (lane8 == row8).astype(F32)

    def block(query, out, grad, logsum):
        products = grad.astype(F32) * out.astype(F32)
        delta = lax.dot_general(
            pick, products, (((1,), (1,)), ((), ())),
            preferred_element_type=F32, precision=lax.Precision.HIGHEST,
        )
        total = None
        for h in range(2):
            qm = head_mask(query, h)
            gm = head_mask(grad, h)
            part = None
            for keys, values, ak, av, text in ((ki, vi, aki, avi, False), (kt, vt, akt, avt, True)):
                scores = dot_nt(keys[...], qm) * (SCALE * LOG2) - logsum[h : h + 1]
                prob = jnp.exp2(scores)
                if text:
                    place = lax.broadcasted_iota(jnp.int32, prob.shape, 0)
                    prob = jnp.where(place < TXT, prob, 0.0)
                grads = (prob * (dot_nt(values[...], gm) - delta[h : h + 1])).astype(BF)
                av[...] += product(prob.astype(BF), gm)
                ak[...] += product(grads, qm)
                term = dot_tn(grads, keys[...])
                part = term if part is None else part + term
            part = head_mask(part, h)
            total = part if total is None else total + part
        return (total * SCALE).astype(BF)

    for b in range(IMG // 256):
        at = pl.ds(b * 256, 256)
        dqi[at, :] = block(qi[at, :], oi[at, :], gi[at, :], li[0, :, at])
    dqt[...] = block(qt[...], ot[...], gt[...], lt[0])
    dki[...] = (aki[...] * SCALE).astype(BF)
    dvi[...] = avi[...].astype(BF)
    dkt[...] = (akt[...] * SCALE).astype(BF)
    dvt[...] = avt[...].astype(BF)


def attend_back(qkv_i, qkv_t, out_i, out_t, grad_i, grad_t, log_i, log_t):
    width = qkv_i.shape[1] // 3
    pairs = width // 128

    def part(rows, which):
        return pl.BlockSpec((rows, 128), lambda j: (0, which * pairs + j))

    results = pl.pallas_call(
        attend_back_kernel,
        grid=(pairs,),
        in_specs=[part(n, w) for n in (IMG, PAD) for w in range(3)]
        + [part(n, 0) for n in (IMG, PAD, IMG, PAD)]
        + [pl.BlockSpec((1, 8, n), lambda j: (j, 0, 0)) for n in (IMG, PAD)],
        out_specs=[part(n, 0) for n in (IMG, PAD) for w in range(3)],
        out_shape=[jax.ShapeDtypeStruct((n, width), BF) for n in (IMG, PAD) for w in range(3)],
        scratch_shapes=[pltpu.VMEM((n, 128), F32) for n in (IMG, IMG, PAD, PAD)],
        compiler_params=pltpu.CompilerParams(vmem_limit_bytes=56 * 1024 * 1024),
        cost_estimate=cost(32),
        name="attend_back",
    )(qkv_i, qkv_i, qkv_i, qkv_t, qkv_t, qkv_t, out_i, out_t, grad_i, grad_t, log_i, log_t)
    return jnp.concatenate(results[:3], axis=1), jnp.concatenate(results[3:], axis=1)


MESH = pl.DeviceIdType.MESH


def cost(micros):
    return pl.CostEstimate(flops=0, bytes_accessed=micros * 3_500_000, transcendentals=0)


def span(start, size):
    unit = 16 if size % 16 == 0 else 8
    return pl.ds(pl.multiple_of(start, unit), size)


class AllGatherCol:
    def __init__(self, value, pieces=1):
        self.ins = [value]
        n, w = value.shape
        self.n, self.pieces, self.step = n, pieces, n // pieces
        self.outs = [jax.ShapeDtypeStruct((4 * n, w), value.dtype)]
        self.scratch = [pltpu.SemaphoreType.DMA((3 * pieces,)) for _ in range(2)]

    def peers(self, me):
        return [(me[0], me[1], me[2] ^ 1), (me[0], me[1], me[2] ^ 2)]

    greets = awaits = peers

    def move(self, refs, me, which, i):
        (value,), (out,), (send, recv) = refs
        core, across = self.peers(me)
        owner = me[2] ^ 2 if which == 2 else me[2]
        slot = out.at[span(owner * self.n + i * self.step, self.step)]
        source = slot if which == 2 else value.at[pl.ds(i * self.step, self.step)]
        k = which * self.pieces + i
        return pltpu.make_async_remote_copy(
            source, slot, send.at[k], recv.at[k],
            device_id=across if which == 0 else core, device_id_type=MESH,
        )

    def start(self, refs, me):
        for which in range(2):
            for i in range(self.pieces):
                self.move(refs, me, which, i).start()
        (value,), (out,), _ = refs
        out[span(me[2] * self.n, self.n)] = value[...]

    def middle(self, refs, me):
        for i in range(self.pieces):
            self.move(refs, me, 0, i).wait_recv()
            self.move(refs, me, 2, i).start()

    def finish(self, refs, me):
        for which in range(3):
            for i in range(self.pieces):
                move = self.move(refs, me, which, i)
                move.wait_send()
                if which:
                    move.wait_recv()


class ReduceScatterCol:
    def __init__(self, value, pieces=1):
        self.ins = [value]
        n, w = value.shape[0] // 4, value.shape[1]
        self.n, self.pieces, self.step = n, pieces, n // pieces
        self.outs = [jax.ShapeDtypeStruct((n, w), F32)]
        self.scratch = [pltpu.VMEM((n, w), BF) for _ in range(4)]
        self.scratch += [pltpu.SemaphoreType.DMA((3 * pieces,)) for _ in range(2)]

    peers = AllGatherCol.peers
    greets = awaits = peers

    def move(self, refs, me, which, i):
        (part,), _, (first, second, third, total, send, recv) = refs
        core, across = self.peers(me)
        at = pl.ds(i * self.step, self.step)
        if which == 2:
            source, target = total.at[at], third.at[at]
        else:
            owner = me[2] ^ 3 if which == 0 else me[2] ^ 1
            source = part.at[span(owner * self.n + i * self.step, self.step)]
            target = (first, second)[which].at[at]
        k = which * self.pieces + i
        return pltpu.make_async_remote_copy(
            source, target, send.at[k], recv.at[k],
            device_id=across if which == 2 else core, device_id_type=MESH,
        )

    def start(self, refs, me):
        for which in range(2):
            for i in range(self.pieces):
                self.move(refs, me, which, i).start()

    def middle(self, refs, me):
        (part,), _, (first, second, third, total, send, recv) = refs
        for i in range(self.pieces):
            self.move(refs, me, 0, i).wait_recv()
            at = pl.ds(i * self.step, self.step)
            mine = part[span((me[2] ^ 2) * self.n + i * self.step, self.step)]
            total[at] = (mine.astype(F32) + first[at].astype(F32)).astype(BF)
            self.move(refs, me, 2, i).start()

    def finish(self, refs, me):
        (part,), (out,), (first, second, third, total, send, recv) = refs
        for i in range(self.pieces):
            for which in (1, 2):
                self.move(refs, me, which, i).wait_recv()
            at = pl.ds(i * self.step, self.step)
            mine = part[span(me[2] * self.n + i * self.step, self.step)].astype(F32)
            out[at] = mine + second[at].astype(F32) + third[at].astype(F32)
        for which in range(3):
            for i in range(self.pieces):
                self.move(refs, me, which, i).wait_send()


class AllGatherRow:
    axis = 1

    def __init__(self, value, size=4):
        self.ins = [value]
        n, w = value.shape
        self.n, self.size = n, size
        self.outs = [jax.ShapeDtypeStruct((size * n, w), value.dtype)]
        self.scratch = [pltpu.SemaphoreType.DMA((size - 1,)) for _ in range(2)]

    def peers(self, me):
        found = []
        for k in range(1, self.size):
            device = list(me)
            device[self.axis] = lax.rem(me[self.axis] + k, self.size)
            found.append(tuple(device))
        return found

    greets = awaits = peers

    def move(self, refs, me, k):
        (value,), (out,), (send, recv) = refs
        return pltpu.make_async_remote_copy(
            value, out.at[span(me[self.axis] * self.n, self.n)], send.at[k], recv.at[k],
            device_id=self.peers(me)[k], device_id_type=MESH,
        )

    def start(self, refs, me):
        for k in range(self.size - 1):
            self.move(refs, me, k).start()
        (value,), (out,), _ = refs
        out[span(me[self.axis] * self.n, self.n)] = value[...]

    def middle(self, refs, me):
        pass

    def finish(self, refs, me):
        for k in range(self.size - 1):
            self.move(refs, me, k).wait()


class AllGatherDp(AllGatherRow):
    axis = 0


class ReduceScatterRow:
    def __init__(self, value):
        self.ins = [value]
        n, w = value.shape[0] // 4, value.shape[1]
        self.n = n
        self.outs = [jax.ShapeDtypeStruct((n, w), F32)]
        self.scratch = [pltpu.VMEM((3, n, w), BF)]
        self.scratch += [pltpu.SemaphoreType.DMA((3,)) for _ in range(2)]

    axis, size = 1, 4
    peers = AllGatherRow.peers
    greets = awaits = peers

    def move(self, refs, me, k):
        (part,), _, (held, send, recv) = refs
        target = self.peers(me)[k]
        return pltpu.make_async_remote_copy(
            part.at[span(target[1] * self.n, self.n)], held.at[k], send.at[k], recv.at[k],
            device_id=target, device_id_type=MESH,
        )

    def start(self, refs, me):
        for k in (1, 0, 2):
            self.move(refs, me, k).start()

    def middle(self, refs, me):
        pass

    def finish(self, refs, me):
        (part,), (out,), (held, send, recv) = refs
        for k in range(3):
            self.move(refs, me, k).wait()
        total = part[span(me[1] * self.n, self.n)].astype(F32)
        for k in range(3):
            total = total + held[k].astype(F32)
        out[...] = total


class ToSequence:
    def __init__(self, value):
        self.ins = [value]
        self.n, self.w = value.shape[0] // 4, value.shape[1]
        self.outs = [jax.ShapeDtypeStruct((self.n, 4 * self.w), value.dtype)]
        self.scratch = [pltpu.SemaphoreType.DMA((4,)) for _ in range(2)]

    def targets(self, me):
        return [(me[0], me[2], k) for k in range(4)]

    def sources(self, me):
        return [(me[0], k, me[1]) for k in range(4)]

    def greets(self, me):
        return [
            (device, jnp.logical_not((device[1] == me[1]) & (device[2] == me[2])))
            for device in self.sources(me)
        ]

    def awaits(self, me):
        return self.targets(me)

    def remote(self, me, device):
        return jnp.logical_not((device[1] == me[1]) & (device[2] == me[2]))

    def place(self, refs, me, k):
        (value,), (out,), _ = refs
        source = value.at[pl.ds(k * self.n, self.n)]
        return source, out.at[:, pl.ds(pl.multiple_of(me[1] * self.w, 128), self.w)]

    def outgoing(self, refs, me, k):
        send, recv = refs[2]
        source, target = self.place(refs, me, k)
        return pltpu.make_async_remote_copy(
            source, target, send.at[k], recv.at[me[1]],
            device_id=self.targets(me)[k], device_id_type=MESH,
        )

    def incoming(self, refs, me, k):
        send, recv = refs[2]
        (value,), (out,), _ = refs
        landing = out.at[:, pl.ds(k * self.w, self.w)]
        return pltpu.make_async_remote_copy(
            value.at[pl.ds(0, self.n)], landing, send.at[k], recv.at[k],
            device_id=self.targets(me)[k], device_id_type=MESH,
        )

    def copy_own(self, refs, me):
        (value,), (out,), _ = refs
        at = pl.ds(pl.multiple_of(me[1] * self.w, 128), self.w)
        out[:, at] = value[span(me[2] * self.n, self.n)]

    def start(self, refs, me):
        for k in range(4):
            @pl.when(self.remote(me, self.targets(me)[k]))
            def _():
                self.outgoing(refs, me, k).start()

        @pl.when(me[1] == me[2])
        def _():
            self.copy_own(refs, me)

    def middle(self, refs, me):
        pass

    def finish(self, refs, me):
        for k in range(4):
            @pl.when(self.remote(me, self.targets(me)[k]))
            def _():
                self.outgoing(refs, me, k).wait_send()

            @pl.when(self.remote(me, self.sources(me)[k]))
            def _():
                self.incoming(refs, me, k).wait_recv()


class FromSequence(ToSequence):
    def __init__(self, value):
        self.ins = [value]
        self.n, self.w = value.shape[0], value.shape[1] // 4
        self.outs = [jax.ShapeDtypeStruct((4 * self.n, self.w), value.dtype)]
        self.scratch = [pltpu.SemaphoreType.DMA((4,)) for _ in range(2)]

    def targets(self, me):
        return [(me[0], k, me[1]) for k in range(4)]

    def sources(self, me):
        return [(me[0], me[2], k) for k in range(4)]

    def outgoing(self, refs, me, k):
        (value,), (out,), (send, recv) = refs
        return pltpu.make_async_remote_copy(
            value.at[:, pl.ds(k * self.w, self.w)],
            out.at[span(me[2] * self.n, self.n)],
            send.at[k], recv.at[me[2]],
            device_id=self.targets(me)[k], device_id_type=MESH,
        )

    def incoming(self, refs, me, k):
        (value,), (out,), (send, recv) = refs
        return pltpu.make_async_remote_copy(
            value.at[:, pl.ds(0, self.w)],
            out.at[pl.ds(k * self.n, self.n)],
            send.at[k], recv.at[k],
            device_id=self.targets(me)[k], device_id_type=MESH,
        )

    def copy_own(self, refs, me):
        (value,), (out,), _ = refs
        at = pl.ds(pl.multiple_of(me[1] * self.w, 128), self.w)
        out[span(me[2] * self.n, self.n)] = value[:, at]


def exchange_kernel(ops, *refs):
    me = tuple(lax.axis_index(name) for name in ("dp", "row", "col"))
    refs = list(refs)
    parts = []
    for kind in ("ins", "outs", "scratch"):
        taken = []
        for op in ops:
            count = len(getattr(op, kind))
            taken.append(refs[:count])
            refs = refs[count:]
        parts.append(taken)
    parts = list(zip(*parts))
    barrier = pltpu.get_barrier_semaphore()
    count = 0
    for op in ops:
        for item in op.greets(me):
            device, wanted = item if len(item) == 2 else (item, None)
            if wanted is None:
                pl.semaphore_signal(barrier, 1, device_id=device, device_id_type=MESH)
            else:
                @pl.when(wanted)
                def _():
                    pl.semaphore_signal(barrier, 1, device_id=device, device_id_type=MESH)
        if isinstance(op, ToSequence):
            count = count + 4 - (me[1] == me[2]).astype(jnp.int32)
        else:
            count = count + len(op.awaits(me))
    pl.semaphore_wait(barrier, count)
    for op, part in zip(ops, parts):
        op.start(part, me)
    for op, part in zip(ops, parts):
        op.middle(part, me)
    for op, part in zip(ops, parts):
        op.finish(part, me)


def exchange(number, micros, *ops):
    ins = [value for op in ops for value in op.ins]
    outs = [shape for op in ops for shape in op.outs]
    results = pl.pallas_call(
        functools.partial(exchange_kernel, ops),
        in_specs=[pl.BlockSpec(memory_space=pltpu.VMEM)] * len(ins),
        out_specs=[pl.BlockSpec(memory_space=pltpu.VMEM)] * len(outs),
        out_shape=outs,
        scratch_shapes=[shape for op in ops for shape in op.scratch],
        compiler_params=pltpu.CompilerParams(
            collective_id=number, has_side_effects=True, vmem_limit_bytes=60 * 1024 * 1024
        ),
        cost_estimate=cost(micros),
        name="exchange" + str(number),
    )(*ins)
    return results if len(results) > 1 else results[0]


def pad_text(values):
    return jnp.pad(values, ((0, PAD - TXT), (0, 0)))


def shards(
    dps,
    rows,
    cols,
    image_tokens,
    text_tokens,
    condition,
    ada_w,
    ada_b,
    qkv_w,
    qkv_b,
    out_w,
    out_b,
    up_w,
    up_b,
    down_w,
    down_b,
    image_cot,
    text_cot,
):
    row = lax.axis_index("row")
    col = lax.axis_index("col")
    seqs = condition.shape[0]
    wr = image_tokens.shape[1]
    wc = condition.shape[1]
    wf = up_w.shape[2]

    parity = lax.rem(lax.axis_index("dp"), 2)
    first_0 = gather_block(
        jnp.concatenate([qkv_w[0].reshape(wr, 3 * wc), out_w[0]], axis=1), dps, parity
    )
    qkv_0 = first_0[:, :, : 3 * wc].reshape(rows * wr, 3 * wc)
    out_0 = first_0[:, :, 3 * wc :].transpose(1, 0, 2).reshape(wc, rows * wr)
    qkv_1 = qkv_w[1].reshape(wr, 3 * wc)
    share = wf // rows
    up_bias_1 = lax.dynamic_slice_in_dim(up_b[1], row * share, share).astype(F32)

    cond_value = condition.astype(F32)
    silu_low = jax.nn.silu(cond_value).astype(BF)
    modul_parts = jnp.concatenate(
        [product(silu_low, ada_w[s].reshape(wc, 6 * wr)) for s in range(2)]
    )
    modul_all = exchange(1, 7, AllGatherCol(modul_parts)).reshape(cols, 2, seqs, 6, wr)
    mods = jnp.sum(modul_all, axis=0) + ada_b.astype(F32)[:, None]
    bias_rows = jnp.broadcast_to(
        jnp.stack([out_b[0], down_b[0]]).astype(F32)[None], (seqs, 2, wr)
    )
    sent = jnp.concatenate([mods[0], bias_rows], axis=1).reshape(seqs * 8, wr)
    x1 = pad_text(text_tokens.astype(F32))
    cot1 = pad_text(text_cot.astype(F32))
    x0, mods_row, stats = exchange(
        2,
        30,
        ToSequence(image_tokens),
        AllGatherRow(sent),
        AllGatherRow(row_stats(x1, x1 * x1)),
    )
    mod_0 = lax.dynamic_index_in_dim(
        mods_row.reshape(rows, seqs, 8, wr), row, 1, keepdims=False
    ).transpose(1, 0, 2).reshape(8, rows * wr)
    mod_1 = lax.dynamic_index_in_dim(mods[1], col, 0, keepdims=False)
    up_0 = gather_block(up_w[0], dps, parity).reshape(rows * wr, wf)

    x0 = x0.astype(F32)
    norm1_0, inv1_0 = norm_local(x0)
    mixed1_0 = (norm1_0 * (1.0 + mod_0[1]) + mod_0[0]).astype(BF)
    norm1_1, inv1_1 = norm_row(x1, stats)
    mixed1_1 = (norm1_1 * (1.0 + mod_1[1]) + mod_1[0]).astype(BF)
    full1_1, full1_0, cot0 = exchange(
        3, 27, AllGatherCol(mixed1_1), AllGatherCol(mixed1_0, 4), ToSequence(image_cot)
    )
    down_0 = gather_block(down_w[0], dps, parity)
    down_0 = down_0.transpose(1, 0, 2).reshape(wf, rows * wr)
    cot0 = cot0.astype(F32)
    qkv_bias = jnp.stack(
        [qkv_b[:, 0], jnp.zeros_like(qkv_b[:, 0]), qkv_b[:, 1]], axis=1
    ).astype(F32).reshape(2, 3 * wc)
    qkv_t, wide_g1, branch_g0 = exchange(
        4,
        45,
        ReduceScatterRow(product(full1_1, qkv_1).astype(BF)),
        AllGatherRow((mod_1[5] * cot1).astype(BF)),
        AllGatherCol((mod_0[5] * cot0).astype(BF), 4),
    )
    text_w = jnp.stack([up_w[1].T.reshape(rows, 2, -1, wr), down_w[1].reshape(rows, 2, -1, wr)])
    text_w = lax.dynamic_index_in_dim(after(text_w, qkv_t), parity, 2, keepdims=False)
    text_w = lax.all_to_all(text_w, "row", 1, 1)
    text_w = in_order(text_w, partner(text_w, dps), parity, 2).reshape(2, rows, -1, wr)
    up_1, down_1 = text_w.transpose(0, 2, 1, 3).reshape(2, -1, rows * wr)
    qkv_txt = (qkv_t + qkv_bias[1]).astype(BF)
    qkv_img = (product(full1_0, qkv_0) + qkv_bias[0]).astype(BF)
    attn_0, attn_text, log_0, log_1 = attend(qkv_img, qkv_txt)
    attn_1, branch_g1 = exchange(
        6, 14, AllGatherRow(attn_text), AllGatherCol(side(wide_g1, rows), 2)
    )

    proj_1, proj_0 = exchange(
        7,
        25,
        ReduceScatterCol(product(attn_1, out_w[1]).astype(BF)),
        ReduceScatterCol(product(attn_0, out_0).astype(BF), 4),
    )
    proj_0 = proj_0 + mod_0[6]
    resid_0 = x0 + mod_0[2] * proj_0
    norm2_0, inv2_0 = norm_local(resid_0)
    mixed2_0 = (norm2_0 * (1.0 + mod_0[4]) + mod_0[3]).astype(BF)
    proj_1 = proj_1 + out_b[1].astype(F32)
    resid_1 = x1 + mod_1[2] * proj_1
    stats, full2_0 = exchange(
        8, 22, AllGatherRow(row_stats(resid_1, resid_1 * resid_1)), AllGatherCol(mixed2_0, 4)
    )
    norm2_1, inv2_1 = norm_row(resid_1, stats)
    mixed2_1 = (norm2_1 * (1.0 + mod_1[4]) + mod_1[3]).astype(BF)
    wide2_1 = exchange(9, 13, AllGatherRow(mixed2_1))
    full2_1 = exchange(10, 13, AllGatherCol(side(wide2_1, rows), 2))

    def halves(values, which):
        cut = values.reshape(values.shape[0], -1, 2, values.shape[1] // 2 // rows)
        return lax.dynamic_index_in_dim(cut, which, 2, keepdims=False).reshape(
            values.shape[0], -1
        )

    def half(values, which):
        cut = values.shape[1] // 2
        return lax.dynamic_slice_in_dim(values, which * cut, cut, 1)

    def by_row(left, right):
        wide = product_left(right, left).reshape(rows, wr, left.shape[1])
        return wide.transpose(0, 2, 1)

    pre_0 = product(full2_0, up_0) + up_b[0].astype(F32)
    hidden_0 = gelu_value(pre_0).astype(BF)
    pre_g0 = gelu_slope(pre_0, product_right(branch_g0, down_0)).astype(BF)
    pre_1 = product_right(full2_1, up_1) + up_bias_1
    hidden_1 = gelu_value(pre_1).astype(BF)
    pre_g1 = gelu_slope(pre_1, product_right(branch_g1, down_1)).astype(BF)

    def add_partner(other, mine):
        return (mine + partner(other, dps).astype(F32)).astype(BF)

    def reduce_block(both):
        return lax.psum_scatter(both, "row", scatter_dimension=0)

    down_o = by_row(half(hidden_0, 1 - parity), branch_g0).astype(BF)
    up_o = product_left(halves(full2_0, 1 - parity), pre_g0).reshape(rows, -1, wf).astype(BF)
    mixed2_g0, wide2_g1 = exchange(
        11,
        35,
        ReduceScatterCol(after(product_right(pre_g0, up_0).astype(BF), down_o, up_o), 4),
        ReduceScatterCol(product(pre_g1, up_1).astype(BF), 2),
    )
    down_b0 = add_partner(down_o, by_row(half(hidden_0, parity), branch_g0))
    up_b0 = add_partner(
        up_o, product_left(halves(full2_0, parity), pre_g0).reshape(rows, -1, wf)
    )
    def text_part(which):
        parts = [
            product_left(half(pre_g1, which), full2_1),
            product_left(half(hidden_1, which), branch_g1),
        ]
        return jnp.stack(parts).astype(BF)

    text_o = text_part(1 - parity)
    text_m = text_part(parity)

    resid_g0 = cot0 + norm_local_back(mixed2_g0 * (1.0 + mod_0[4]), norm2_0, inv2_0)
    down_h0 = reduce_block(down_b0)
    mixed2_g1, proj_g0 = exchange(
        12,
        22,
        ReduceScatterRow(stack(wide2_g1.astype(BF), rows)),
        AllGatherCol((mod_0[2] * resid_g0).astype(BF), 4),
    )
    up_h0 = reduce_block(up_b0)
    norm2_g1 = mixed2_g1 * (1.0 + mod_1[4])
    stats, wide_1 = exchange(
        13,
        16,
        AllGatherRow(row_stats(norm2_g1, norm2_g1 * norm2_1)),
        ReduceScatterCol(after(product(hidden_1, down_1).astype(BF), down_b0), 2),
    )
    resid_g1 = cot1 + norm_row_back(norm2_g1, norm2_1, inv2_1, stats)
    proj_g1 = exchange(14, 7, AllGatherCol((mod_1[2] * resid_g1).astype(BF)))
    attn_g0 = product_right(proj_g0, out_0).astype(BF)
    attn_g1, branch_0 = exchange(
        15,
        22,
        ReduceScatterRow(product_right(proj_g1, out_w[1]).astype(BF)),
        ReduceScatterCol(product(hidden_0, down_0).astype(BF), 4),
    )
    attn_g1 = attn_g1.astype(BF)
    branch_0 = branch_0 + mod_0[7]
    out_g1 = product_left(attn_1, proj_g1)
    out_o = by_row(half(attn_0, 1 - parity), proj_g0).astype(BF)
    qkv_grad_0, qkv_grad_t = attend_back(
        qkv_img, qkv_txt, attn_0, attn_text, after(attn_g0, out_o, text_o, up_b0), attn_g1, log_0, log_1
    )
    out_b0 = add_partner(out_o, by_row(half(attn_0, parity), proj_g0))
    out_h0 = reduce_block(out_b0)
    text_b = (text_m + partner(text_o, dps).astype(F32)).astype(BF)
    text_b = text_b.reshape(2, share // 2, rows, wr).transpose(0, 2, 1, 3)
    text_h = lax.all_to_all(text_b, "row", 1, 1)
    qkv_o = product_left(halves(full1_0, 1 - parity), qkv_grad_0)
    qkv_o = qkv_o.reshape(rows, -1, 3 * wc).astype(BF)

    def column_sums(values):
        return jnp.sum(values, axis=0, dtype=F32)

    first = (row == 0).astype(F32)
    place = (lax.iota(jnp.int32, rows) == row).astype(F32)[:, None]
    qkv_s0 = column_sums(qkv_grad_0)
    qkv_s1 = column_sums(qkv_grad_t)
    vectors = jnp.concatenate(
        [
            column_sums(branch_g0),
            column_sums(proj_g0),
            column_sums(branch_g1) * first,
            (place * column_sums(proj_g1)[None]).reshape(-1),
            column_sums(pre_g0),
            (place * column_sums(pre_g1)[None]).reshape(-1),
            qkv_s0[:wc],
            qkv_s0[2 * wc :],
            qkv_s1[:wc],
            qkv_s1[2 * wc :],
        ]
    ).reshape(-1, wc)
    pad_rows = -vectors.shape[0] % 8
    qkv_grad_1, mixed1_g0, vectors = exchange(
        16,
        35,
        AllGatherRow(qkv_grad_t),
        ReduceScatterCol(after(product_right(qkv_grad_0, qkv_0).astype(BF), qkv_o), 4),
        AllGatherRow(jnp.pad(vectors, ((0, pad_rows), (0, 0)))),
    )
    qkv_b0 = add_partner(
        qkv_o, product_left(halves(full1_0, parity), qkv_grad_0).reshape(rows, -1, 3 * wc)
    )
    qkv_g1 = product_left(full1_1, qkv_grad_1)
    image_grad = resid_g0 + norm_local_back(mixed1_g0 * (1.0 + mod_0[1]), norm1_0, inv1_0)
    mixed1_g1, branch_1, vectors, image_grad, image_out = exchange(
        17,
        37,
        ReduceScatterCol(product_right(qkv_grad_1, qkv_1).astype(BF)),
        ReduceScatterRow(stack(after(wide_1, out_b0, down_h0).astype(BF), rows)),
        AllGatherDp(jnp.sum(vectors.reshape(rows, -1, wc), axis=0), dps),
        FromSequence(image_grad.astype(BF)),
        FromSequence((resid_0 + mod_0[5] * branch_0).astype(BF)),
    )
    vectors = jnp.sum(vectors.reshape(dps, -1, wc), axis=0).reshape(-1)
    qkv_h0 = reduce_block(qkv_b0)
    branch_1 = branch_1 + down_b[1].astype(F32)
    text_out = (resid_1 + mod_1[5] * branch_1).astype(BF)[:TXT]
    norm1_g1 = mixed1_g1 * (1.0 + mod_1[1])

    sums_0 = jnp.stack(
        [
            jnp.sum(t, axis=0)
            for t in (
                mixed1_g0,
                mixed1_g0 * norm1_0,
                resid_g0 * proj_0,
                mixed2_g0,
                mixed2_g0 * norm2_0,
                cot0 * branch_0,
            )
        ]
    )
    sums_1 = jnp.stack(
        [
            jnp.sum(t, axis=0)
            for t in (
                mixed1_g1,
                mixed1_g1 * norm1_1,
                resid_g1 * proj_1,
                mixed2_g1,
                mixed2_g1 * norm2_1,
                cot1 * branch_1,
            )
        ]
    )
    stats, cols_0, cols_1 = exchange(
        18,
        10,
        AllGatherRow(row_stats(norm1_g1, norm1_g1 * norm1_1)),
        AllGatherCol(jnp.pad(sums_0, ((0, 2), (0, 0)))),
        AllGatherCol(jnp.pad(sums_1, ((0, 2), (0, 0)))),
    )
    image_grad = image_grad.astype(F32)
    text_grad = resid_g1 + norm_row_back(norm1_g1, norm1_1, inv1_1, stats)
    rows_0 = exchange(19, 8, AllGatherRow(jnp.sum(cols_0.reshape(cols, 8, rows * wr), axis=0)))
    rows_0 = lax.dynamic_index_in_dim(
        rows_0.reshape(seqs, 8, rows, wr)[:, :6], row, 2, keepdims=False
    )
    mods_low = jnp.stack([rows_0, cols_1.reshape(seqs, 8, wr)[:, :6]]).astype(BF)
    mods_low = mods_low.reshape(2, seqs, 6 * wr)
    silu_part = product_right(mods_low[0], ada_w[0].reshape(wc, 6 * wr)) + product_right(
        mods_low[1], ada_w[1].reshape(wc, 6 * wr)
    )
    mods_all, silu_all, silu_part = exchange(
        20,
        9,
        AllGatherDp(mods_low.reshape(2 * seqs, 6 * wr).astype(F32), dps),
        AllGatherDp(jnp.pad(silu_low.astype(F32), ((0, 8 - seqs), (0, 0))), dps),
        AllGatherRow(jnp.pad(silu_part, ((0, 8 - seqs), (0, 0)))),
    )
    mods_all = mods_all.reshape(dps, 2, seqs, 6 * wr).transpose(1, 0, 2, 3)
    mods_all = mods_all.reshape(2, dps * seqs, 6 * wr).astype(BF)
    silu_all = silu_all.reshape(dps, 8, wc)[:, :seqs].reshape(dps * seqs, wc).astype(BF)
    ada_gw = jnp.stack(
        [product_left(silu_all, mods_all[s]).reshape(wc, 6, wr) for s in range(2)]
    )
    ada_gb = jnp.sum(mods_all, axis=1, dtype=F32).reshape(2, 6, wr)
    silu_sum = jnp.sum(silu_part.reshape(rows, 8, wc), axis=0)[:seqs]
    condition_grad = silu_slope(cond_value, silu_sum)
    row_sums = lax.dynamic_index_in_dim(
        vectors[: 4 * rows * wr].reshape(2, 2, rows, wr), row, 2, keepdims=False
    )
    rest = vectors[4 * rows * wr : 4 * rows * wr + 2 * wf + 4 * wc]
    up_gb = rest[: 2 * wf].reshape(2, wf)
    qkv_gb = rest[2 * wf :].reshape(2, 2, wc)

    def finish(half_sum, second_part):
        first_part = join_over_dp(half_sum, dps, parity)
        return jnp.stack([first_part, sum_over_dp(second_part.astype(BF), dps)])

    text_h = text_h.transpose(2, 0, 1, 3)
    text_g = join_over_dp(text_h[None], dps, parity)
    text_g = text_g.reshape(2, share // 2, 2, rows, wr).transpose(2, 3, 0, 1, 4).reshape(2, wf, wr)
    up_g = jnp.stack([join_over_dp(up_h0, dps, parity), text_g[0].T])
    down_g = jnp.stack([join_over_dp(down_h0, dps, parity), text_g[1]])

    return (
        image_out,
        text_out,
        image_grad,
        text_grad[:TXT],
        condition_grad,
        ada_gw,
        ada_gb,
        finish(qkv_h0, qkv_g1).reshape(2, wr, 3, wc),
        qkv_gb,
        finish(out_h0, out_g1),
        row_sums[:, 1],
        up_g,
        up_gb,
        down_g,
        row_sums[:, 0],
    )


def solution(mesh):
    placed = (
        P(("dp", "col"), "row"),
        P(("dp", "col"), "row"),
        P("dp", "col"),
        P(None, "col", None, "row"),
        P(None, None, "row"),
        P(None, "row", None, "col"),
        P(None, None, "col"),
        P(None, "col", "row"),
        P(None, "row"),
        P(None, "row", "col"),
        P(None, "col"),
        P(None, "col", "row"),
        P(None, "row"),
        P(("dp", "col"), "row"),
        P(("dp", "col"), "row"),
    )
    sizes = [mesh.shape[name] for name in ("dp", "row", "col")]
    return jax.shard_map(
        functools.partial(shards, *sizes),
        mesh=mesh,
        in_specs=placed,
        out_specs=(
            P(("dp", "col"), "row"),
            P(("dp", "col"), "row"),
            P(("dp", "col"), "row"),
            P(("dp", "col"), "row"),
            P("dp", "col"),
            P(None, "col", None, "row"),
            P(None, None, "row"),
            P(None, "row", None, "col"),
            P(None, None, "col"),
            P(None, "col", "row"),
            P(None, "row"),
            P(None, "row", "col"),
            P(None, "col"),
            P(None, "col", "row"),
            P(None, "row"),
        ),
        check_vma=False,
    )
```

```python
import functools

import jax
import jax.numpy as jnp
from jax import lax
from jax.experimental import pallas as pl
from jax.experimental.pallas import tpu as pltpu
from jax.sharding import PartitionSpec as P

D = 1536
HEAD = 64
IMG = 1024
TXT = 154
PAD = 160
SCALE = HEAD**-0.5
EPSILON = 1e-06
BF = jnp.bfloat16
F32 = jnp.float32


def product(left, right):
    return jnp.dot(left, right, preferred_element_type=F32)


def product_left(left, right):
    return lax.dot_general(left, right, (((0,), (0,)), ((), ())), preferred_element_type=F32)


def product_right(left, right):
    return lax.dot_general(left, right, (((1,), (1,)), ((), ())), preferred_element_type=F32)


def gelu_value(values):
    return jax.nn.gelu(values, approximate=True)


def gelu_slope(values, grad):
    return jax.vjp(gelu_value, values)[1](grad)[0]


def silu_slope(values, grad):
    return jax.vjp(jax.nn.silu, values)[1](grad)[0]


def gather(values, axis_name, axis=0):
    return lax.all_gather(values, axis_name, axis=axis, tiled=True)


def sum_pair(mine_first, dps):
    if dps == 2:
        return SumPair(mine_first.reshape(-1, mine_first.shape[2])), lambda values: values[0]
    total = lax.psum(mine_first, "dp")
    half = lax.dynamic_index_in_dim(total, lax.rem(lax.axis_index("dp"), 2), 0, False)
    return Body(lambda: None, [], []), lambda values: half


class Weight:
    def __init__(self, block, axis):
        self.block, self.axis = block, axis
        self.parity = lax.rem(lax.axis_index("dp"), 2)

    def cut(self, which):
        return lax.dynamic_slice_in_dim(self.block, which * 384, 384, self.axis)

    def gather(self, i, *earlier):
        mine = after(self.cut(2 * self.parity + i), *earlier)
        return lax.all_gather(mine, "row", tiled=True)

    def other(self, i):
        return self.cut(2 * (1 - self.parity) + i)

    def swap(self, i, gathered):
        return SwapBlocks(gathered, self.other(i))


def reduce_row(values):
    values = values.reshape(4, -1, values.shape[1])
    return lax.psum_scatter(values, "row", scatter_dimension=0)


def after(value, *others):
    return lax.optimization_barrier((value, others))[0]


def norm_local(values):
    mean = jnp.mean(values, axis=1, keepdims=True)
    square = jnp.mean(values * values, axis=1, keepdims=True)
    inverse = lax.rsqrt(square - mean * mean + EPSILON)
    return (values - mean) * inverse, inverse


def norm_local_back(grad, normed, inverse):
    total = jnp.mean(grad, axis=1, keepdims=True)
    cross = jnp.mean(grad * normed, axis=1, keepdims=True)
    return inverse * (grad - total - normed * cross)


def row_stats(first, second):
    pair = jnp.stack([jnp.sum(first, axis=1), jnp.sum(second, axis=1)])
    return jnp.pad(pair, ((0, 6), (0, 0)))


def row_means(stats):
    totals = jnp.sum(stats.reshape(4, 8, -1)[:, :2], axis=0) / D
    return totals[0][:, None], totals[1][:, None]


def norm_row(values, stats):
    mean, square = row_means(stats)
    inverse = lax.rsqrt(square - mean * mean + EPSILON)
    return (values - mean) * inverse, inverse


def norm_row_back(grad, normed, inverse, stats):
    total, cross = row_means(stats)
    return inverse * (grad - total - normed * cross)


def side(values, rows):
    width = values.shape[1]
    return values.reshape(rows, -1, width).transpose(1, 0, 2).reshape(-1, rows * width)


def stack(values, rows):
    count = values.shape[0]
    return values.reshape(count, rows, -1).transpose(1, 0, 2).reshape(rows * count, -1)


LOG2 = 1.4426950408889634


def dot_nt(left, right):
    return lax.dot_general(left, right, (((1,), (1,)), ((), ())), preferred_element_type=F32)


def dot_tn(left, right):
    return lax.dot_general(left, right, (((0,), (0,)), ((), ())), preferred_element_type=F32)


def head_mask(values, head):
    lane = lax.broadcasted_iota(jnp.int32, values.shape, 1)
    return jnp.where((lane >= head * HEAD) & (lane < (head + 1) * HEAD), values, 0)


def attend_body(pairs, full_i, full_t, oi, ot, li, lt, kim, vim, ktm, vtm):
    def pair(p, carry):
        at_q, at_k, at_v = (lanes((which * pairs + p) * 128, 128) for which in range(3))
        for h in range(2):
            kim[h] = head_mask(full_i[:, at_k], h)
            vim[h] = head_mask(full_i[:, at_v], h)
            ktm[h] = head_mask(full_t[:, at_k], h)
            vtm[h] = head_mask(full_t[:, at_v], h)

        def block(query):
            total = None
            rows = []
            for h in range(2):
                si = dot_nt(query, kim[h])
                st = dot_nt(query, ktm[h])
                lane = lax.broadcasted_iota(jnp.int32, st.shape, 1)
                st = jnp.where(lane < TXT, st, -1e30)
                peak = jnp.maximum(
                    jnp.max(si, axis=1, keepdims=True), jnp.max(st, axis=1, keepdims=True)
                )
                ei = jnp.exp2((si - peak) * (SCALE * LOG2))
                et = jnp.exp2((st - peak) * (SCALE * LOG2))
                norm = jnp.sum(ei, axis=1, keepdims=True) + jnp.sum(et, axis=1, keepdims=True)
                part = product(ei.astype(BF), vim[h]) + product(et.astype(BF), vtm[h])
                part = part / norm
                total = part if total is None else total + part
                rows.append(peak * (SCALE * LOG2) + jnp.log2(norm))
            lane = lax.broadcasted_iota(jnp.int32, total.shape, 1)
            stats = jnp.where(lane == 0, rows[0], jnp.where(lane == 1, rows[1], 0.0))
            return total.astype(BF), jnp.transpose(stats)[:8]

        for b in range(IMG // 256):
            at = pl.ds(b * 256, 256)
            oi[at, at_q], li[p, :, at] = block(full_i[at, at_q])
        ot[:, at_q], lt[p] = block(full_t[:, at_q])
        return carry

    lax.fori_loop(0, pairs, pair, 0)


def attend(qkv_i, qkv_t):
    width = qkv_i.shape[1] // 3
    pairs = width // 128
    return Body(
        functools.partial(attend_body, pairs),
        [qkv_i, qkv_t],
        [
            jax.ShapeDtypeStruct((IMG, width), BF),
            jax.ShapeDtypeStruct((PAD, width), BF),
            jax.ShapeDtypeStruct((pairs, 8, IMG), F32),
            jax.ShapeDtypeStruct((pairs, 8, PAD), F32),
        ],
        [pltpu.VMEM((2, n, 128), BF) for n in (IMG, IMG, PAD, PAD)],
    )


def attend_back_body(
    pairs, full_i, full_t, oi, ot, gi, gt, li, lt, di, dt, aki, avi, akt, avt
):
    lane8 = lax.broadcasted_iota(jnp.int32, (8, 128), 1) // HEAD
    row8 = lax.broadcasted_iota(jnp.int32, (8, 128), 0)
    pick = (lane8 == row8).astype(F32)

    def pair(p, carry):
        at_q, at_k, at_v = (lanes((which * pairs + p) * 128, 128) for which in range(3))
        for acc in (aki, avi, akt, avt):
            acc[...] = jnp.zeros_like(acc)

        def block(query, out, grad, logsum):
            products = grad.astype(F32) * out.astype(F32)
            delta = lax.dot_general(
                pick, products, (((1,), (1,)), ((), ())),
                preferred_element_type=F32, precision=lax.Precision.HIGHEST,
            )
            total = None
            for h in range(2):
                qm = head_mask(query, h)
                gm = head_mask(grad, h)
                part = None
                for full, ak, av, text in ((full_i, aki, avi, False), (full_t, akt, avt, True)):
                    keys, values = full[:, at_k], full[:, at_v]
                    scores = dot_nt(keys, qm) * (SCALE * LOG2) - logsum[h : h + 1]
                    prob = jnp.exp2(scores)
                    if text:
                        place = lax.broadcasted_iota(jnp.int32, prob.shape, 0)
                        prob = jnp.where(place < TXT, prob, 0.0)
                    grads = (prob * (dot_nt(values, gm) - delta[h : h + 1])).astype(BF)
                    av[...] += product(prob.astype(BF), gm)
                    ak[...] += product(grads, qm)
                    term = dot_tn(grads, keys)
                    part = term if part is None else part + term
                part = head_mask(part, h)
                total = part if total is None else total + part
            return (total * SCALE).astype(BF)

        for b in range(IMG // 256):
            at = pl.ds(b * 256, 256)
            di[at, at_q] = block(full_i[at, at_q], oi[at, at_q], gi[at, at_q], li[p, :, at])
        dt[:, at_q] = block(full_t[:, at_q], ot[:, at_q], gt[:, at_q], lt[p])
        di[:, at_k] = (aki[...] * SCALE).astype(BF)
        di[:, at_v] = avi[...].astype(BF)
        dt[:, at_k] = (akt[...] * SCALE).astype(BF)
        dt[:, at_v] = avt[...].astype(BF)
        return carry

    lax.fori_loop(0, pairs, pair, 0)


def attend_back(qkv_i, qkv_t, out_i, out_t, grad_i, grad_t, log_i, log_t):
    pairs = qkv_i.shape[1] // 384
    return Body(
        functools.partial(attend_back_body, pairs),
        [qkv_i, qkv_t, out_i, out_t, grad_i, grad_t, log_i, log_t],
        [jax.ShapeDtypeStruct(v.shape, BF) for v in (qkv_i, qkv_t)],
        [pltpu.VMEM((n, 128), F32) for n in (IMG, IMG, PAD, PAD)],
    )


MESH = pl.DeviceIdType.MESH


def lanes(start, size):
    return pl.ds(pl.multiple_of(start, 128), size)


def cost(micros):
    return pl.CostEstimate(flops=0, bytes_accessed=micros * 3_500_000, transcendentals=0)


def span(start, size):
    unit = 16 if size % 16 == 0 else 8
    return pl.ds(pl.multiple_of(start, unit), size)


class AllGatherCol:
    def __init__(self, value, pieces=1):
        self.ins = [value]
        n, w = value.shape
        self.n, self.pieces, self.step = n, pieces, n // pieces
        self.outs = [jax.ShapeDtypeStruct((4 * n, w), value.dtype)]
        self.scratch = [pltpu.SemaphoreType.DMA((3 * pieces,)) for _ in range(2)]

    def peers(self, me):
        return [(me[0], me[1], me[2] ^ 1), (me[0], me[1], me[2] ^ 2)]

    greets = awaits = peers

    def move(self, refs, me, which, i):
        (value,), (out,), (send, recv) = refs
        core, across = self.peers(me)
        owner = me[2] ^ 2 if which == 2 else me[2]
        slot = out.at[span(owner * self.n + i * self.step, self.step)]
        source = slot if which == 2 else value.at[pl.ds(i * self.step, self.step)]
        k = which * self.pieces + i
        return pltpu.make_async_remote_copy(
            source, slot, send.at[k], recv.at[k],
            device_id=across if which == 0 else core, device_id_type=MESH,
        )

    def start(self, refs, me):
        for which in range(2):
            for i in range(self.pieces):
                self.move(refs, me, which, i).start()
        (value,), (out,), _ = refs
        out[span(me[2] * self.n, self.n)] = value[...]

    def middle(self, refs, me):
        for i in range(self.pieces):
            self.move(refs, me, 0, i).wait_recv()
            self.move(refs, me, 2, i).start()

    def wait_core(self, refs, me):
        for i in range(self.pieces):
            self.move(refs, me, 1, i).wait_recv()

    def finish(self, refs, me, core=True):
        if core:
            self.wait_core(refs, me)
        for which in range(3):
            for i in range(self.pieces):
                move = self.move(refs, me, which, i)
                move.wait_send()
                if which == 2:
                    move.wait_recv()


class ReduceScatterCol:
    def __init__(self, value, pieces=1):
        self.ins = [value]
        n, w = value.shape[0] // 4, value.shape[1]
        self.n, self.pieces, self.step = n, pieces, n // pieces
        self.outs = [jax.ShapeDtypeStruct((n, w), F32)]
        self.scratch = [pltpu.VMEM((n, w), BF) for _ in range(4)]
        self.scratch += [pltpu.SemaphoreType.DMA((3 * pieces,)) for _ in range(2)]

    peers = AllGatherCol.peers
    greets = awaits = peers

    def move(self, refs, me, which, i):
        (part,), _, (first, second, third, total, send, recv) = refs
        core, across = self.peers(me)
        at = pl.ds(i * self.step, self.step)
        if which == 2:
            source, target = total.at[at], third.at[at]
        else:
            owner = me[2] ^ 3 if which == 0 else me[2] ^ 1
            source = part.at[span(owner * self.n + i * self.step, self.step)]
            target = (first, second)[which].at[at]
        k = which * self.pieces + i
        return pltpu.make_async_remote_copy(
            source, target, send.at[k], recv.at[k],
            device_id=across if which == 2 else core, device_id_type=MESH,
        )

    def start(self, refs, me):
        for which in range(2):
            for i in range(self.pieces):
                self.move(refs, me, which, i).start()

    def middle(self, refs, me):
        (part,), _, (first, second, third, total, send, recv) = refs
        for i in range(self.pieces):
            self.move(refs, me, 0, i).wait_recv()
            at = pl.ds(i * self.step, self.step)
            mine = part[span((me[2] ^ 2) * self.n + i * self.step, self.step)]
            total[at] = (mine.astype(F32) + first[at].astype(F32)).astype(BF)
            self.move(refs, me, 2, i).start()

    def finish(self, refs, me):
        (part,), (out,), (first, second, third, total, send, recv) = refs
        for i in range(self.pieces):
            for which in (1, 2):
                self.move(refs, me, which, i).wait_recv()
            at = pl.ds(i * self.step, self.step)
            mine = part[span(me[2] * self.n + i * self.step, self.step)].astype(F32)
            out[at] = mine + second[at].astype(F32) + third[at].astype(F32)
        for which in range(3):
            for i in range(self.pieces):
                self.move(refs, me, which, i).wait_send()


class AllGatherRow:
    axis = 1

    def __init__(self, value, size=4):
        self.ins = [value]
        n, w = value.shape
        self.n, self.size = n, size
        self.outs = [jax.ShapeDtypeStruct((size * n, w), value.dtype)]
        self.scratch = [pltpu.SemaphoreType.DMA((size - 1,)) for _ in range(2)]

    def peers(self, me):
        found = []
        for k in range(1, self.size):
            device = list(me)
            device[self.axis] = lax.rem(me[self.axis] + k, self.size)
            found.append(tuple(device))
        return found

    greets = awaits = peers

    def move(self, refs, me, k):
        (value,), (out,), (send, recv) = refs
        return pltpu.make_async_remote_copy(
            value, out.at[span(me[self.axis] * self.n, self.n)], send.at[k], recv.at[k],
            device_id=self.peers(me)[k], device_id_type=MESH,
        )

    def start(self, refs, me):
        for k in range(self.size - 1):
            self.move(refs, me, k).start()
        (value,), (out,), _ = refs
        out[span(me[self.axis] * self.n, self.n)] = value[...]

    def middle(self, refs, me):
        pass

    def finish(self, refs, me):
        for k in range(self.size - 1):
            self.move(refs, me, k).wait()


class AllGatherDp(AllGatherRow):
    axis = 0


class AllToAllRow(AllGatherRow):
    def __init__(self, value):
        self.ins = [value]
        self.n, self.size = value.shape[0] // 4, 4
        self.outs = [jax.ShapeDtypeStruct(value.shape, value.dtype)]
        self.scratch = [pltpu.SemaphoreType.DMA((3,)) for _ in range(2)]

    def move(self, refs, me, k):
        (value,), (out,), (send, recv) = refs
        target = self.peers(me)[k]
        return pltpu.make_async_remote_copy(
            value.at[span(target[1] * self.n, self.n)],
            out.at[span(me[1] * self.n, self.n)],
            send.at[k], recv.at[k],
            device_id=target, device_id_type=MESH,
        )

    def start(self, refs, me):
        for k in range(3):
            self.move(refs, me, k).start()
        (value,), (out,), _ = refs
        at = span(me[1] * self.n, self.n)
        out[at] = value[at]


class SwapBlocks:
    def __init__(self, value, own):
        self.ins = [value, own]
        self.n = own.shape[0]
        self.outs = [jax.ShapeDtypeStruct((2 * value.shape[0], value.shape[1]), value.dtype)]
        self.scratch = [pltpu.SemaphoreType.DMA((3,)) for _ in range(2)]

    def peers(self, me):
        return [(me[0] ^ 1, me[1], me[2])]

    greets = awaits = peers

    def move(self, refs, me, k):
        (value, own), (out,), (send, recv) = refs
        block = lax.rem(me[1] + k + 1, 4)
        place = (lax.rem(me[0], 2) * 4 + block) * self.n
        return pltpu.make_async_remote_copy(
            value.at[span(block * self.n, self.n)], out.at[span(place, self.n)],
            send.at[k], recv.at[k],
            device_id=self.peers(me)[0], device_id_type=MESH,
        )

    def start(self, refs, me):
        for k in range(3):
            self.move(refs, me, k).start()
        (value, own), (out,), _ = refs
        parity = lax.rem(me[0], 2)
        out[span(parity * 4 * self.n, 4 * self.n)] = value[...]
        out[span(((1 - parity) * 4 + me[1]) * self.n, self.n)] = own[...]

    def middle(self, refs, me):
        pass

    def finish(self, refs, me):
        for k in range(3):
            self.move(refs, me, k).wait()


class SumPair:
    def __init__(self, value):
        self.ins = [value]
        n, w = value.shape[0] // 2, value.shape[1]
        self.n = n
        self.outs = [jax.ShapeDtypeStruct((n, w), BF)]
        self.scratch = [pltpu.VMEM((n, w), BF)]
        self.scratch += [pltpu.SemaphoreType.DMA((1,)) for _ in range(2)]

    def peers(self, me):
        return [(1 - me[0], me[1], me[2])]

    greets = awaits = peers

    def move(self, refs, me):
        (part,), _, (held, send, recv) = refs
        return pltpu.make_async_remote_copy(
            part.at[span((1 - me[0]) * self.n, self.n)], held, send.at[0], recv.at[0],
            device_id=self.peers(me)[0], device_id_type=MESH,
        )

    def start(self, refs, me):
        self.move(refs, me).start()

    def middle(self, refs, me):
        pass

    def finish(self, refs, me):
        (part,), (out,), (held, send, recv) = refs
        self.move(refs, me).wait()
        mine = part[span(me[0] * self.n, self.n)].astype(F32)
        out[...] = (mine + held[...].astype(F32)).astype(BF)


class ReduceScatterRow:
    def __init__(self, value):
        self.ins = [value]
        n, w = value.shape[0] // 4, value.shape[1]
        self.n = n
        self.outs = [jax.ShapeDtypeStruct((n, w), F32)]
        self.scratch = [pltpu.VMEM((3, n, w), BF)]
        self.scratch += [pltpu.SemaphoreType.DMA((3,)) for _ in range(2)]

    axis, size = 1, 4
    peers = AllGatherRow.peers
    greets = awaits = peers

    def move(self, refs, me, k):
        (part,), _, (held, send, recv) = refs
        target = self.peers(me)[k]
        return pltpu.make_async_remote_copy(
            part.at[span(target[1] * self.n, self.n)], held.at[k], send.at[k], recv.at[k],
            device_id=target, device_id_type=MESH,
        )

    def start(self, refs, me):
        for k in (1, 0, 2):
            self.move(refs, me, k).start()

    def middle(self, refs, me):
        pass

    def finish(self, refs, me):
        (part,), (out,), (held, send, recv) = refs
        for k in range(3):
            self.move(refs, me, k).wait()
        total = part[span(me[1] * self.n, self.n)].astype(F32)
        for k in range(3):
            total = total + held[k].astype(F32)
        out[...] = total


class ToSequence:
    def __init__(self, value):
        self.ins = [value]
        self.n, self.w = value.shape[0] // 4, value.shape[1]
        self.outs = [jax.ShapeDtypeStruct((self.n, 4 * self.w), value.dtype)]
        self.scratch = [pltpu.SemaphoreType.DMA((4,)) for _ in range(2)]

    def targets(self, me):
        return [(me[0], me[2], k) for k in range(4)]

    def sources(self, me):
        return [(me[0], k, me[1]) for k in range(4)]

    def greets(self, me):
        return [
            (device, jnp.logical_not((device[1] == me[1]) & (device[2] == me[2])))
            for device in self.sources(me)
        ]

    def awaits(self, me):
        return self.targets(me)

    def remote(self, me, device):
        return jnp.logical_not((device[1] == me[1]) & (device[2] == me[2]))

    def place(self, refs, me, k):
        (value,), (out,), _ = refs
        source = value.at[pl.ds(k * self.n, self.n)]
        return source, out.at[:, pl.ds(pl.multiple_of(me[1] * self.w, 128), self.w)]

    def outgoing(self, refs, me, k):
        send, recv = refs[2]
        source, target = self.place(refs, me, k)
        return pltpu.make_async_remote_copy(
            source, target, send.at[k], recv.at[me[1]],
            device_id=self.targets(me)[k], device_id_type=MESH,
        )

    def incoming(self, refs, me, k):
        send, recv = refs[2]
        (value,), (out,), _ = refs
        landing = out.at[:, pl.ds(k * self.w, self.w)]
        return pltpu.make_async_remote_copy(
            value.at[pl.ds(0, self.n)], landing, send.at[k], recv.at[k],
            device_id=self.targets(me)[k], device_id_type=MESH,
        )

    def copy_own(self, refs, me):
        (value,), (out,), _ = refs
        at = pl.ds(pl.multiple_of(me[1] * self.w, 128), self.w)
        out[:, at] = value[span(me[2] * self.n, self.n)]

    def start(self, refs, me):
        for k in range(4):
            @pl.when(self.remote(me, self.targets(me)[k]))
            def _():
                self.outgoing(refs, me, k).start()

        @pl.when(me[1] == me[2])
        def _():
            self.copy_own(refs, me)

    def middle(self, refs, me):
        pass

    def finish(self, refs, me):
        for k in range(4):
            @pl.when(self.remote(me, self.targets(me)[k]))
            def _():
                self.outgoing(refs, me, k).wait_send()

            @pl.when(self.remote(me, self.sources(me)[k]))
            def _():
                self.incoming(refs, me, k).wait_recv()


class FromSequence(ToSequence):
    def __init__(self, value):
        self.ins = [value]
        self.n, self.w = value.shape[0], value.shape[1] // 4
        self.outs = [jax.ShapeDtypeStruct((4 * self.n, self.w), value.dtype)]
        self.scratch = [pltpu.SemaphoreType.DMA((4,)) for _ in range(2)]

    def targets(self, me):
        return [(me[0], k, me[1]) for k in range(4)]

    def sources(self, me):
        return [(me[0], me[2], k) for k in range(4)]

    def outgoing(self, refs, me, k):
        (value,), (out,), (send, recv) = refs
        return pltpu.make_async_remote_copy(
            value.at[:, pl.ds(k * self.w, self.w)],
            out.at[span(me[2] * self.n, self.n)],
            send.at[k], recv.at[me[2]],
            device_id=self.targets(me)[k], device_id_type=MESH,
        )

    def incoming(self, refs, me, k):
        (value,), (out,), (send, recv) = refs
        return pltpu.make_async_remote_copy(
            value.at[:, pl.ds(0, self.w)],
            out.at[pl.ds(k * self.n, self.n)],
            send.at[k], recv.at[k],
            device_id=self.targets(me)[k], device_id_type=MESH,
        )

    def copy_own(self, refs, me):
        (value,), (out,), _ = refs
        at = pl.ds(pl.multiple_of(me[1] * self.w, 128), self.w)
        out[span(me[2] * self.n, self.n)] = value[:, at]


class Body:
    def __init__(self, work, ins, outs, scratch=()):
        self.work, self.ins, self.outs, self.scratch = work, list(ins), list(outs), list(scratch)


def exchange_kernel(ops, *refs):
    me = tuple(lax.axis_index(name) for name in ("dp", "row", "col"))
    refs = list(refs)
    parts = []
    for kind in ("ins", "outs", "scratch"):
        taken = []
        for op in ops:
            count = len(getattr(op, kind))
            taken.append(refs[:count])
            refs = refs[count:]
        parts.append(taken)
    parts = list(zip(*parts))
    moving = [(op, part) for op, part in zip(ops, parts) if not isinstance(op, Body)]
    barrier = pltpu.get_barrier_semaphore()
    count = 0
    for op, _ in moving:
        for item in op.greets(me):
            device, wanted = item if len(item) == 2 else (item, None)
            if wanted is None:
                pl.semaphore_signal(barrier, 1, device_id=device, device_id_type=MESH)
            else:
                @pl.when(wanted)
                def _():
                    pl.semaphore_signal(barrier, 1, device_id=device, device_id_type=MESH)
        if isinstance(op, ToSequence):
            count = count + 4 - (me[1] == me[2]).astype(jnp.int32)
        else:
            count = count + len(op.awaits(me))
    pl.semaphore_wait(barrier, count)
    for op, part in moving:
        op.start(part, me)
    for op, part in zip(ops, parts):
        if isinstance(op, Body):
            op.work(*part[0], *part[1], *part[2])
    for op, part in moving:
        op.middle(part, me)
    for op, part in moving:
        op.finish(part, me)


def exchange(number, micros, *ops, name="exchange"):
    ins = [value for op in ops for value in op.ins]
    outs = [shape for op in ops for shape in op.outs]
    results = pl.pallas_call(
        functools.partial(exchange_kernel, ops),
        in_specs=[pl.BlockSpec(memory_space=pltpu.VMEM)] * len(ins),
        out_specs=[pl.BlockSpec(memory_space=pltpu.VMEM)] * len(outs),
        out_shape=outs,
        scratch_shapes=[shape for op in ops for shape in op.scratch],
        compiler_params=pltpu.CompilerParams(
            collective_id=number, has_side_effects=True, vmem_limit_bytes=60 * 1024 * 1024
        ),
        cost_estimate=cost(micros),
        name=name + str(number),
    )(*ins)
    return results


def gelu_pair(values):
    inner = 0.7978845608028654 * (values + 0.044715 * values * values * values)
    bend = jnp.tanh(inner)
    half = 0.5 * (1.0 + bend)
    slope = half + values * (0.5 * (1.0 - bend * bend)) * (
        0.7978845608028654 * (1.0 + 0.134145 * values * values)
    )
    return values * half, slope


def block_copies(target, parts, sems, first, by_rows):
    copies = []
    for i, part in enumerate(parts):
        for k in range(2):
            for r in range(4):
                source = part.at[pl.ds((k * 4 + r) * 384, 384)]
                along, cross = pl.ds(r * 384, 384), pl.ds((2 * k + i) * 384, 384)
                place = target.at[cross, along] if by_rows else target.at[along, cross]
                copies.append(pltpu.make_async_copy(source, place, sems.at[first]))
                first += 1
    return copies


def input_kernel(x, part_a, part_b, bias, qkv, qkv_w, out_w, weight, sems):
    copies = block_copies(weight, (part_a, part_b), sems, 0, False)
    for copy in copies:
        copy.start()
    for copy in copies:
        copy.wait()
    width = qkv.shape[1]
    back = [pltpu.make_async_copy(weight.at[:, pl.ds(0, width)], qkv_w, sems.at[0])]
    for r in range(4):
        back.append(
            pltpu.make_async_copy(
                weight.at[pl.ds(r * 384, 384), pl.ds(width, 384)],
                out_w.at[:, pl.ds(r * 384, 384)],
                sems.at[1 + r],
            )
        )
    for copy in back:
        copy.start()

    def step(i, _):
        at = lanes(i * 384, 384)
        qkv[:, at] = (product(x[...], weight[:, at]) + bias[:, at]).astype(BF)
        return _

    lax.fori_loop(0, width // 384, step, 0)
    for copy in back:
        copy.wait()


def input_product(x, parts, bias):
    rows, depth = x.shape
    width = 3 * 384
    return pl.pallas_call(
        input_kernel,
        in_specs=[
            pl.BlockSpec(memory_space=pltpu.VMEM),
            *[pl.BlockSpec(memory_space=pl.ANY)] * 2,
            pl.BlockSpec(memory_space=pltpu.VMEM),
        ],
        out_specs=[
            pl.BlockSpec(memory_space=pltpu.VMEM),
            pl.BlockSpec(memory_space=pl.ANY),
            pl.BlockSpec(memory_space=pl.ANY),
        ],
        out_shape=[
            jax.ShapeDtypeStruct((rows, width), BF),
            jax.ShapeDtypeStruct((depth, width), BF),
            jax.ShapeDtypeStruct((384, depth), BF),
        ],
        scratch_shapes=[pltpu.VMEM((depth, 1536), BF), pltpu.SemaphoreType.DMA((16,))],
        compiler_params=pltpu.CompilerParams(vmem_limit_bytes=56 * 1024 * 1024),
        cost_estimate=cost(8),
        name="input_product",
    )(x, *parts, bias)


def feed_kernel(ops, me, refs):
    gather_0, sums_t, gather_r, gather_t, scatter_0, scatter_t, scatter_b, *swaps = ops
    ins, outs, scratch = refs
    (mixed_0, resid_t, mod_t, grad_0, grad_t, bias_0, bias_t) = ins[:7]
    (down_a, own_a, down_b, own_b, up_a, up_b, text_p) = ins[7:]
    (mixed_g0, wide_g1, stats_out, sum_0, sum_t, branch_0) = outs[:6]
    (gup, gdown, gtext, branch_t) = outs[6:]
    (full_0, up, down, hidden, pre_g, part_0, stage, text_w) = scratch[:8]
    (stats_in, mixed_t, wide_t, side_t, full_t, hidden_t, pre_gt, part_t) = scratch[8:16]
    (w_sems, s_sems, part_b, down_all) = scratch[16:20]
    rest = scratch[20:]
    dp, row, col = me
    refs_g0 = ((mixed_0,), (full_0,), rest[0:2])
    refs_st = ((stats_in,), (stats_out,), rest[2:4])
    refs_gr = ((mixed_t,), (wide_t,), rest[4:6])
    refs_gt = ((side_t,), (full_t,), rest[6:8])
    refs_s0 = ((part_0,), (mixed_g0,), rest[8:14])
    refs_s1 = ((part_t,), (wide_g1,), rest[14:20])
    refs_sb = ((part_b,), (branch_0,), rest[20:26])
    refs_sd = [
        ((down_a, own_a), (down_all.at[0],), rest[26:28]),
        ((down_b, own_b), (down_all.at[1],), rest[28:30]),
    ]

    for i, swap in enumerate(swaps):
        swap.start(refs_sd[i], me)
    copies = block_copies(up, (up_a, up_b), w_sems, 0, False)
    parity = lax.rem(dp, 2)
    for k in range(2):
        for r in range(4):
            for w in range(2):
                at = text_w.at[w, pl.ds(k * 192, 192), pl.ds(r * 384, 384)]
                source = text_p.at[pl.ds((k * 4 + r) * 384 + w * 192, 192)]
                copies.append(pltpu.make_async_copy(source, at, w_sems.at[16 + 8 * k + 2 * r + w]))
    for copy in copies:
        copy.start()
    gather_0.start(refs_g0, me)

    resid = resid_t[...]
    lane = lax.broadcasted_iota(jnp.int32, (PAD, 128), 1)
    pair = jnp.where(
        lane == 0,
        jnp.sum(resid, axis=1, keepdims=True),
        jnp.where(lane == 1, jnp.sum(resid * resid, axis=1, keepdims=True), 0.0),
    )
    stats_in[...] = jnp.transpose(pair)[:8]
    sums_t.start(refs_st, me)
    sums_t.finish(refs_st, me)
    total = stats_out[0:8] + stats_out[8:16] + stats_out[16:24] + stats_out[24:32]
    total = jnp.transpose(jnp.concatenate([total, jnp.zeros((120, PAD), F32)], axis=0)) / D
    mean, square = total[:, 0:1], total[:, 1:2]
    normed = (resid - mean) * lax.rsqrt(square - mean * mean + EPSILON)
    mixed_t[...] = (normed * mod_t[1:2] + mod_t[0:1]).astype(BF)
    gather_r.start(refs_gr, me)
    for copy in copies:
        copy.wait()
    for i, swap in enumerate(swaps):
        swap.finish(refs_sd[i], me)
        for k in range(2):
            for r in range(4):
                place = down.at[pl.ds((2 * k + i) * 384, 384), pl.ds(r * 384, 384)]
                place[...] = down_all[i, pl.ds((k * 4 + r) * 384, 384), :]
    sum_0[...] = jnp.zeros_like(sum_0)
    sum_t[...] = jnp.zeros_like(sum_t)

    def quarter(i, carry):
        @pl.when(i == 2)
        def _():
            gather_r.finish(refs_gr, me)
            for r in range(4):
                side_t[:, pl.ds(r * 384, 384)] = wide_t[pl.ds(r * PAD, PAD), :]
            gather_0.middle(refs_g0, me)
            gather_0.finish(refs_g0, me, False)
            gather_t.start(refs_gt, me)

        @pl.when(i == 1)
        def _():
            gather_0.wait_core(refs_g0, me)

        at = span((col ^ (i ^ (i // 2))) * 256, 256)

        def tile(j, carry):
            cut = lanes(j * 512, 512)
            pre = product(full_0[at, :], up[:, cut]) + bias_0[:, cut]
            value, slope = gelu_pair(pre)
            hidden[at, cut] = value.astype(BF)
            back = product_right(grad_0[at, :], down[cut, :])
            grad = (back * slope).astype(BF)
            pre_g[at, cut] = grad
            sum_0[:, cut] += jnp.sum(grad.astype(F32), axis=0, keepdims=True)
            return carry

        lax.fori_loop(0, 3, tile, 0)

        def tile_back(j, carry):
            cut = lanes(j * 512, 512)
            part_0[at, cut] = product_right(pre_g[at, :], up[cut, :]).astype(BF)
            return carry

        lax.fori_loop(0, 3, tile_back, 0)
        return carry

    lax.fori_loop(0, 4, quarter, 0)
    scatter_0.start(refs_s0, me)
    scatter_0.middle(refs_s0, me)
    gather_t.middle(refs_gt, me)
    gather_t.finish(refs_gt, me)

    def text_quarter(i, carry):
        at = span(i * PAD, PAD)
        pre = product_right(full_t[at, :], text_w[0]) + bias_t[...]
        value, slope = gelu_pair(pre)
        hidden_t[at, :] = value.astype(BF)
        grad = (product_right(grad_t[at, :], text_w[1]) * slope).astype(BF)
        pre_gt[at, :] = grad
        sum_t[...] += jnp.sum(grad.astype(F32), axis=0, keepdims=True)
        part_t[at, :] = product(grad, text_w[0]).astype(BF)
        return carry

    lax.fori_loop(0, 4, text_quarter, 0)
    scatter_t.start(refs_s1, me)
    scatter_t.middle(refs_s1, me)

    def branch_quarter(i, carry):
        at = span(i * 256, 256)
        for j in range(3):
            cut = pl.ds(j * 512, 512)
            part_b[at, cut] = product(hidden[at, :], down[:, cut]).astype(BF)
        return carry

    lax.fori_loop(0, 4, branch_quarter, 0)
    scatter_b.start(refs_sb, me)
    scatter_b.middle(refs_sb, me)

    def put(slot, moves):
        for k, (source, target) in enumerate(moves):
            pltpu.make_async_copy(source, target, s_sems.at[slot, k]).start()

    def done(slot, moves):
        for k, (source, target) in enumerate(moves):
            pltpu.make_async_copy(source, target, s_sems.at[slot, k]).wait()

    def staged(count, value_of, moves_of):
        def step(i, carry):
            slot = lax.rem(i, 2)

            @pl.when(i >= 2)
            def _():
                done(slot, moves_of(i - 2, stage.at[slot]))

            value_of(i, stage.at[slot])
            put(slot, moves_of(i, stage.at[slot]))
            return carry

        lax.fori_loop(0, count, step, 0)
        for i in (count - 2, count - 1):
            done(i % 2, moves_of(i, stage.at[i % 2]))

    def value_of(i, place):
        cut = lanes(i * 384, 384)
        for j in range(3):
            at = pl.ds(j * 512, 512)
            place[:, at] = product_left(hidden[:, cut], grad_0[:, at]).astype(BF)

    def moves_of(i, place):
        return [
            (
                place.at[:, pl.ds(r * 384, 384)],
                gdown.at[lax.rem(i, 2), i // 2, r],
            )
            for r in range(4)
        ]

    staged(4, value_of, moves_of)

    def value_of(i, place):
        for j in range(3):
            at = pl.ds(j * 512, 512)
            left = full_0[:, lanes(i * 384, 384)]
            place[:, at] = product_left(left, pre_g[:, at]).astype(BF)

    def moves_of(i, place):
        return [
            (place.at[:, pl.ds((2 * k + q) * 384, 384)], gup.at[q, k, i])
            for k in range(2)
            for q in range(2)
        ]

    staged(4, value_of, moves_of)

    def value_of(i, place):
        @pl.when(i == 0)
        def _():
            for j in range(3):
                at = pl.ds(j * 512, 512)
                place[:, at] = product_left(pre_gt[...], full_t[:, at]).astype(BF)

        @pl.when(i == 1)
        def _():
            for j in range(3):
                at = pl.ds(j * 512, 512)
                place[:, at] = product_left(hidden_t[...], grad_t[:, at]).astype(BF)

    def moves_of(i, place):
        return [
            (place.at[pl.ds(k * 192, 192)], gtext.at[i, k]) for k in range(2)
        ]

    staged(2, value_of, moves_of)

    def value_of(i, place):
        at = span(i * PAD, PAD)
        place[pl.ds(0, PAD)] = product(hidden_t[at, :], text_w[1]).astype(BF)

    def moves_of(i, place):
        return [(place.at[pl.ds(0, PAD)], branch_t.at[span(i * PAD, PAD)])]

    staged(4, value_of, moves_of)
    scatter_0.finish(refs_s0, me)
    scatter_t.finish(refs_s1, me)
    scatter_b.finish(refs_sb, me)


def feed(number, mixed_0, resid_t, mod_t, grad_0, grad_t, bias_0, bias_t, *weights):
    def shape(*dims, dtype=BF):
        return jax.ShapeDtypeStruct(dims, dtype)

    ops = (
        AllGatherCol(mixed_0, 4),
        AllGatherRow(shape(8, PAD, dtype=F32)),
        AllGatherRow(shape(PAD, 384)),
        AllGatherCol(shape(PAD, 1536), 2),
        ReduceScatterCol(shape(1024, 1536), 4),
        ReduceScatterCol(shape(640, 1536), 2),
        ReduceScatterCol(shape(1024, 1536), 4),
        SwapBlocks(weights[0], weights[1]),
        SwapBlocks(weights[2], weights[3]),
    )

    def kernel(*refs):
        me = tuple(lax.axis_index(name) for name in ("dp", "row", "col"))
        barrier = pltpu.get_barrier_semaphore()
        peers = ops[0].peers(me) + ops[1].peers(me) + ops[-1].peers(me)
        for device in peers:
            pl.semaphore_signal(barrier, 1, device_id=device, device_id_type=MESH)
        pl.semaphore_wait(barrier, len(peers))
        feed_kernel(ops, me, (refs[:14], refs[14:24], refs[24:]))

    outs = [
        shape(256, 1536, dtype=F32),
        shape(PAD, 1536, dtype=F32),
        shape(32, PAD, dtype=F32),
        shape(1, 1536, dtype=F32),
        shape(1, 384, dtype=F32),
        shape(256, 1536, dtype=F32),
        shape(2, 2, 4, 384, 384),
        shape(2, 2, 4, 384, 384),
        shape(2, 2, 192, 1536),
        shape(640, 1536),
    ]
    vmem, hbm = pl.BlockSpec(memory_space=pltpu.VMEM), pl.BlockSpec(memory_space=pl.ANY)
    return pl.pallas_call(
        kernel,
        in_specs=[vmem] * 11 + [hbm] * 3,
        out_specs=[vmem] * 6 + [hbm] * 4,
        out_shape=outs,
        scratch_shapes=[
            pltpu.VMEM((1024, 1536), BF),
            pltpu.VMEM((1536, 1536), BF),
            pltpu.VMEM((1536, 1536), BF),
            pltpu.VMEM((1024, 1536), BF),
            pltpu.VMEM((1024, 1536), BF),
            pltpu.VMEM((1024, 1536), BF),
            pltpu.VMEM((2, 384, 1536), BF),
            pltpu.VMEM((2, 384, 1536), BF),
            pltpu.VMEM((8, PAD), F32),
            pltpu.VMEM((PAD, 384), BF),
            pltpu.VMEM((640, 384), BF),
            pltpu.VMEM((PAD, 1536), BF),
            pltpu.VMEM((640, 1536), BF),
            pltpu.VMEM((640, 384), BF),
            pltpu.VMEM((640, 384), BF),
            pltpu.VMEM((640, 1536), BF),
            pltpu.SemaphoreType.DMA((40,)),
            pltpu.SemaphoreType.DMA((2, 4)),
            pltpu.VMEM((1024, 1536), BF),
            pltpu.VMEM((2, 3072, 384), BF),
        ]
        + [item for op in ops for item in op.scratch],
        compiler_params=pltpu.CompilerParams(
            collective_id=number, has_side_effects=True, vmem_limit_bytes=62 * 1024 * 1024
        ),
        cost_estimate=cost(90),
        name="feed",
    )(mixed_0, resid_t, mod_t, grad_0, grad_t, bias_0, bias_t, *weights)


class SumPairFar(SumPair):
    def __init__(self, value):
        super().__init__(value)
        self.scratch.append(pltpu.SemaphoreType.DMA((1,)))

    def move(self, refs, me):
        return SumPair.move(self, (refs[0], refs[1], refs[2][:3]), me)

    def finish(self, refs, me):
        (part,), (out,), (held, send, recv, local) = refs
        mine = pltpu.make_async_copy(part.at[span(me[0] * self.n, self.n)], out, local.at[0])
        mine.start()
        mine.wait()
        self.move(refs, me).wait()
        out[...] = (out[...].astype(F32) + held[...].astype(F32)).astype(BF)


def columns(rows):
    return jnp.transpose(jnp.concatenate([rows, jnp.zeros((120, PAD), F32)], axis=0))


def row_total(gathered):
    return gathered[0:8] + gathered[8:16] + gathered[16:24] + gathered[24:32]


def back_kernel(plan, me, refs):
    ins, outs, scratch = refs
    named, sums, pairs = plan
    (gmixed_0, cot_0, resid_0, mod_0, stacked_t, cot_t, resid_t, stats_2, mod_t) = ins[:9]
    (out_0, out_1, image_seq, qkv_i, qkv_t, attn_i, attn_t, log_i, log_t) = ins[9:18]
    text_in, far = ins[18], ins[19:]
    (gresid_0, proj_0, gmixed_t, gresid_t, proj_t, image_out, dqkv_i, dqkv_t, text_out) = outs[:9]
    far_out = outs[9:]
    (own_0, own_t, stats_in, stats_all, part_t, gattn_t32, gattn_i, gattn_t) = scratch[:8]
    (text_sum, text_stack, aki, avi, akt, avt) = scratch[8:14]
    rest = list(scratch[14:])

    def take(op):
        count = len(op.scratch)
        found = rest[:count]
        del rest[:count]
        return found

    io = {
        "reduce_t": ((stacked_t,), (gmixed_t,)),
        "gather_0": ((own_0,), (proj_0,)),
        "stats": ((stats_in,), (stats_all,)),
        "gather_t": ((own_t,), (proj_t,)),
        "reduce_a": ((part_t,), (gattn_t32,)),
        "image": ((image_seq,), (image_out,)),
        "text": ((text_stack,), (text_out,)),
    }
    refs_of = {key: (*io[key], take(op)) for key, op in named.items()}
    sum_refs = [((text_in,), (text_sum,), take(op)) for op in sums]
    far_refs = [((far[i],), (far_out[i],), take(op)) for i, op in enumerate(pairs)]

    def do(key, step):
        getattr(named[key], step)(refs_of[key], me)

    do("reduce_t", "start")
    for op, part in zip(sums, sum_refs):
        op.start(part, me)

    def norm_rows(i, carry):
        at = pl.ds(pl.multiple_of(i * 64, 64), 64)
        resid = resid_0[at, :]
        mean = jnp.mean(resid, axis=1, keepdims=True)
        square = jnp.mean(resid * resid, axis=1, keepdims=True)
        inverse = lax.rsqrt(square - mean * mean + EPSILON)
        normed = (resid - mean) * inverse
        grad = gmixed_0[at, :] * (1.0 + mod_0[4:5])
        total = jnp.mean(grad, axis=1, keepdims=True)
        cross = jnp.mean(grad * normed, axis=1, keepdims=True)
        result = cot_0[at, :].astype(F32) + inverse * (grad - total - normed * cross)
        gresid_0[at, :] = result
        own_0[at, :] = (result * mod_0[2:3]).astype(BF)
        return carry

    lax.fori_loop(0, 4, norm_rows, 0)
    do("gather_0", "start")
    do("reduce_t", "finish")

    before = columns(row_total(stats_2)) / D
    mean, square = before[:, 0:1], before[:, 1:2]
    inverse = lax.rsqrt(square - mean * mean + EPSILON)
    normed = (resid_t[...] - mean) * inverse
    grad = gmixed_t[...] * (1.0 + mod_t[4:5])
    lane = lax.broadcasted_iota(jnp.int32, (PAD, 128), 1)
    pair = jnp.where(
        lane == 0,
        jnp.sum(grad, axis=1, keepdims=True),
        jnp.where(lane == 1, jnp.sum(grad * normed, axis=1, keepdims=True), 0.0),
    )
    stats_in[...] = jnp.transpose(pair)[:8]
    do("stats", "start")
    do("stats", "finish")
    after_sums = columns(row_total(stats_all)) / D
    total, cross = after_sums[:, 0:1], after_sums[:, 1:2]
    result = cot_t[...] + inverse * (grad - total - normed * cross)
    gresid_t[...] = result
    own_t[...] = (result * mod_t[2:3]).astype(BF)
    do("gather_t", "start")
    do("image", "start")
    do("gather_t", "middle")
    do("gather_t", "finish")
    for i in range(4):
        at = pl.ds(i * PAD, PAD)
        part_t[at, :] = product_right(proj_t[at, :], out_1[...]).astype(BF)
    do("reduce_a", "start")
    do("gather_0", "middle")
    for op, part in zip(sums, sum_refs):
        op.finish(part, me)
    for op, part in zip(pairs, far_refs):
        op.start(part, me)
    text = text_sum if sums else text_in
    for r in range(4):
        text_stack[pl.ds(r * 384, 384), :] = text[:, pl.ds(r * 384, 384)]
    do("text", "start")
    do("gather_0", "finish")

    def rows_back(i, carry):
        at = span(i * 256, 256)
        gattn_i[at, :] = product_right(proj_0[at, :], out_0[...]).astype(BF)
        return carry

    lax.fori_loop(0, 4, rows_back, 0)
    do("reduce_a", "finish")
    gattn_t[...] = gattn_t32[...].astype(BF)
    attend_back_body(
        qkv_i.shape[1] // 384,
        qkv_i, qkv_t, attn_i, attn_t, gattn_i, gattn_t, log_i, log_t,
        dqkv_i, dqkv_t, aki, avi, akt, avt,
    )
    do("text", "finish")
    do("image", "finish")
    for op, part in zip(pairs, far_refs):
        op.finish(part, me)


def back(number, dps, values, text, fars):
    def shape(*dims, dtype=BF):
        return jax.ShapeDtypeStruct(dims, dtype)

    named = {
        "reduce_t": ReduceScatterRow(shape(640, 384)),
        "gather_0": AllGatherCol(shape(256, 1536), 4),
        "stats": AllGatherRow(shape(8, PAD, dtype=F32)),
        "gather_t": AllGatherCol(shape(PAD, 384)),
        "reduce_a": ReduceScatterRow(shape(640, 384)),
        "image": FromSequence(shape(256, 1536)),
        "text": AllToAllRow(shape(1536, 384)),
    }
    sums = [SumPair(text)] if dps == 2 else []
    pairs = [SumPairFar(far) for far in fars]
    ops = list(named.values()) + sums + pairs
    count = 19 + len(fars)
    out_shapes = [
        shape(256, 1536, dtype=F32),
        shape(1024, 1536),
        shape(PAD, 384, dtype=F32),
        shape(PAD, 384, dtype=F32),
        shape(640, 384),
        shape(1024, 384),
        shape(1024, 1152),
        shape(PAD, 1152),
        shape(1536, 384),
    ] + [op.outs[0] for op in pairs]

    def kernel(*refs):
        me = tuple(lax.axis_index(name) for name in ("dp", "row", "col"))
        barrier = pltpu.get_barrier_semaphore()
        peers = named["gather_0"].peers(me) + named["stats"].peers(me)
        if dps == 2:
            peers = peers + sums[0].peers(me)
        for device in peers:
            pl.semaphore_signal(barrier, 1, device_id=device, device_id_type=MESH)
        image = named["image"]
        for device, wanted in image.greets(me):
            @pl.when(wanted)
            def _():
                pl.semaphore_signal(barrier, 1, device_id=device, device_id_type=MESH)
        pl.semaphore_wait(barrier, len(peers) + 4 - (me[1] == me[2]).astype(jnp.int32))
        outs = count + len(out_shapes)
        back_kernel((named, sums, pairs), me, (refs[:count], refs[count:outs], refs[outs:]))

    vmem, hbm = pl.BlockSpec(memory_space=pltpu.VMEM), pl.BlockSpec(memory_space=pl.ANY)
    return pl.pallas_call(
        kernel,
        in_specs=[vmem] * 19 + [hbm] * len(fars),
        out_specs=[vmem] * len(out_shapes),
        out_shape=out_shapes,
        scratch_shapes=[
            pltpu.VMEM((256, 1536), BF),
            pltpu.VMEM((PAD, 384), BF),
            pltpu.VMEM((8, PAD), F32),
            pltpu.VMEM((32, PAD), F32),
            pltpu.VMEM((640, 384), BF),
            pltpu.VMEM((PAD, 384), F32),
            pltpu.VMEM((1024, 384), BF),
            pltpu.VMEM((PAD, 384), BF),
            pltpu.VMEM((384, 1536), BF),
            pltpu.VMEM((1536, 384), BF),
        ]
        + [pltpu.VMEM((n, 128), F32) for n in (IMG, IMG, PAD, PAD)]
        + [item for op in ops for item in op.scratch],
        compiler_params=pltpu.CompilerParams(
            collective_id=number, has_side_effects=True, vmem_limit_bytes=62 * 1024 * 1024
        ),
        cost_estimate=cost(130),
        name="back",
    )(*values, text, *fars)


def finish_feed_kernel(up_parts, down_parts, text, up, down):
    for k in range(4):
        at = slice(k * 384, (k + 1) * 384)
        up[0, :, at] = up_parts[at].astype(F32)
        down[0, at] = down_parts[at].astype(F32)
    for r in range(4):
        starts = [k * 1536 + r * 384 for k in range(2)]
        both = [text[start : start + 192].astype(F32) for start in starts]
        up[1, :, r * 384 : (r + 1) * 384] = jnp.transpose(jnp.concatenate(both, axis=0))
        for k in range(2):
            place = r * 384 + k * 192
            down[1, place : place + 192] = text[starts[k] + 192 : starts[k] + 384].astype(F32)


def finish_rest_kernel(dps, parts, qkv_parts, out_parts, qkv, out):
    for k in range(3):
        at = slice(k * 384, (k + 1) * 384)
        qkv[0, :, at] = parts[at].astype(F32)
    out[0] = parts[1152:1536].astype(F32)
    for target, terms in ((qkv, qkv_parts), (out, out_parts)):
        total = terms[0:384].astype(F32)
        for d in range(1, dps):
            total = total + terms[d * 384 : (d + 1) * 384].astype(F32)
        target[1] = total


def finish(kernel, name, shapes, *values):
    return pl.pallas_call(
        kernel,
        in_specs=[pl.BlockSpec(memory_space=pltpu.VMEM)] * len(values),
        out_specs=[pl.BlockSpec(memory_space=pltpu.VMEM)] * len(shapes),
        out_shape=[jax.ShapeDtypeStruct(shape, F32) for shape in shapes],
        compiler_params=pltpu.CompilerParams(vmem_limit_bytes=56 * 1024 * 1024),
        cost_estimate=cost(6),
        name=name,
    )(*values)


def pad_text(values):
    return jnp.pad(values, ((0, PAD - TXT), (0, 0)))


def shards(
    dps,
    rows,
    cols,
    image_tokens,
    text_tokens,
    condition,
    ada_w,
    ada_b,
    qkv_w,
    qkv_b,
    out_w,
    out_b,
    up_w,
    up_b,
    down_w,
    down_b,
    image_cot,
    text_cot,
):
    row = lax.axis_index("row")
    col = lax.axis_index("col")
    seqs = condition.shape[0]
    wr = image_tokens.shape[1]
    wc = condition.shape[1]
    wf = up_w.shape[2]

    first_w = Weight(jnp.concatenate([qkv_w[0].reshape(wr, 3 * wc), out_w[0]], axis=1), 1)
    first_a = first_w.gather(0)
    parity = lax.rem(lax.axis_index("dp"), 2)
    qkv_1 = qkv_w[1].reshape(wr, 3 * wc)
    share = wf // rows
    up_bias_1 = lax.dynamic_slice_in_dim(up_b[1], row * share, share).astype(F32)

    cond_value = condition.astype(F32)
    silu_low = jax.nn.silu(cond_value).astype(BF)
    modul_parts = jnp.concatenate(
        [product(silu_low, ada_w[s].reshape(wc, 6 * wr)) for s in range(2)]
    )
    modul_all = exchange(1, 7, AllGatherCol(modul_parts))[0].reshape(cols, 2, seqs, 6, wr)
    mods = jnp.sum(modul_all, axis=0) + ada_b.astype(F32)[:, None]
    bias_rows = jnp.broadcast_to(
        jnp.stack([out_b[0], down_b[0]]).astype(F32)[None], (seqs, 2, wr)
    )
    sent = jnp.concatenate([mods[0], bias_rows], axis=1).reshape(seqs * 8, wr)
    x1 = pad_text(text_tokens.astype(F32))
    cot1 = pad_text(text_cot.astype(F32))
    x0, mods_row, stats = exchange(
        2,
        30,
        ToSequence(image_tokens),
        AllGatherRow(sent),
        AllGatherRow(row_stats(x1, x1 * x1)),
    )
    mod_0 = lax.dynamic_index_in_dim(
        mods_row.reshape(rows, seqs, 8, wr), row, 1, keepdims=False
    ).transpose(1, 0, 2).reshape(8, rows * wr)
    mod_1 = lax.dynamic_index_in_dim(mods[1], col, 0, keepdims=False)
    first_b = first_w.gather(1, x0)

    x0 = x0.astype(F32)
    norm1_0, inv1_0 = norm_local(x0)
    mixed1_0 = (norm1_0 * (1.0 + mod_0[1]) + mod_0[0]).astype(BF)
    norm1_1, inv1_1 = norm_row(x1, stats)
    mixed1_1 = (norm1_1 * (1.0 + mod_1[1]) + mod_1[0]).astype(BF)
    full1_1, full1_0, cot0 = exchange(
        3,
        27,
        AllGatherCol(mixed1_1),
        AllGatherCol(mixed1_0, 4),
        ToSequence(image_cot),
    )
    cot0 = cot0.astype(F32)
    qkv_bias = jnp.stack(
        [qkv_b[:, 0], jnp.zeros_like(qkv_b[:, 0]), qkv_b[:, 1]], axis=1
    ).astype(F32).reshape(2, 3 * wc)
    first_a, first_b, qkv_t, wide_g1, branch_g0 = exchange(
        4,
        45,
        first_w.swap(0, first_a),
        first_w.swap(1, first_b),
        ReduceScatterRow(product(full1_1, qkv_1).astype(BF)),
        AllGatherRow((mod_1[5] * cot1).astype(BF)),
        AllGatherCol((mod_0[5] * cot0).astype(BF), 4),
    )
    up_0, down_0 = Weight(up_w[0], 1), Weight(down_w[0], 0)
    up_a, up_b0 = up_0.gather(0, qkv_t), up_0.gather(1, qkv_t)
    down_a, down_b0 = down_0.gather(0, qkv_t), down_0.gather(1, qkv_t)
    qkv_txt = (qkv_t + qkv_bias[1]).astype(BF)
    qkv_img, qkv_0, out_0 = input_product(full1_0, [first_a, first_b], qkv_bias[:1])
    text_w = jnp.stack([up_w[1].T.reshape(rows, 2, -1, wr), down_w[1].reshape(rows, 2, -1, wr)])
    text_w, text_own = (
        lax.dynamic_index_in_dim(text_w, half, 2, keepdims=False).transpose(1, 0, 2, 3)
        for half in (parity, 1 - parity)
    )
    text_own = lax.dynamic_index_in_dim(text_own, row, 0, False).reshape(-1, wr)
    attn_0, attn_text, log_0, log_1, text_w = exchange(
        5,
        26,
        attend(qkv_img, qkv_txt),
        AllToAllRow(text_w.reshape(-1, wr)),
        name="attend",
    )
    up_a, attn_1, branch_g1 = exchange(
        6,
        20,
        up_0.swap(0, up_a),
        AllGatherRow(attn_text),
        AllGatherCol(side(wide_g1, rows), 2),
    )

    up_b0, text_w, proj_1, proj_0 = exchange(
        7,
        32,
        up_0.swap(1, up_b0),
        SwapBlocks(text_w, text_own),
        ReduceScatterCol(product(attn_1, out_w[1]).astype(BF)),
        ReduceScatterCol(product(attn_0, out_0).astype(BF), 4),
    )
    proj_0 = proj_0 + mod_0[6]
    resid_0 = x0 + mod_0[2] * proj_0
    norm2_0, inv2_0 = norm_local(resid_0)
    mixed2_0 = (norm2_0 * (1.0 + mod_0[4]) + mod_0[3]).astype(BF)
    proj_1 = proj_1 + out_b[1].astype(F32)
    resid_1 = x1 + mod_1[2] * proj_1
    def by_row(left, right):
        wide = product_left(right, left).reshape(rows, wr, left.shape[1])
        return wide.transpose(0, 2, 1)

    results = feed(
        8,
        mixed2_0,
        resid_1,
        jnp.pad(jnp.stack([mod_1[3], 1.0 + mod_1[4]]), ((0, 6), (0, 0))),
        branch_g0,
        branch_g1,
        up_b[:1].astype(F32),
        up_bias_1[None],
        down_a,
        down_0.other(0),
        down_b0,
        down_0.other(1),
        up_a,
        up_b0,
        text_w,
    )
    mixed2_g0, wide2_g1, stats, pre_s0, pre_s1, branch_0 = results[:6]
    up_p, down_p, text_p, branch_p1 = results[6:]
    branch_0 = branch_0 + mod_0[7]
    norm2_1, inv2_1 = norm_row(resid_1, stats)
    fars = [part.reshape(-1, wr) for part in (down_p[0], down_p[1], up_p[0], up_p[1])]
    text_p = text_p.transpose(1, 0, 2, 3).reshape(-1, rows * wr)
    parity_now = lax.rem(lax.axis_index("dp"), 2)
    if dps != 2:
        halves = [
            lax.dynamic_slice_in_dim(
                lax.psum(part, "dp"), parity_now * (part.shape[0] // 2), part.shape[0] // 2
            )
            for part in fars + [text_p]
        ]
        fars, text_p = [], halves[4]
    (
        resid_g0,
        proj_g0,
        mixed2_g1,
        resid_g1,
        proj_g1,
        image_out,
        qkv_grad_0,
        qkv_grad_t,
        text_h,
        *sums,
    ) = back(
        11,
        dps,
        [
            mixed2_g0,
            cot0.astype(BF),
            resid_0,
            mod_0,
            stack(wide2_g1.astype(BF), rows),
            cot1,
            resid_1,
            stats,
            jnp.pad(mod_1, ((0, 2), (0, 0))),
            out_0,
            out_w[1],
            (resid_0 + mod_0[5] * branch_0).astype(BF),
            qkv_img,
            qkv_txt,
            attn_0,
            attn_text,
            log_0,
            log_1,
        ],
        text_p,
        fars,
    )
    down_ha, down_hb, up_ha, up_hb = [
        reduce_row(part) for part in (sums if dps == 2 else halves[:4])
    ]
    out_g1 = product_left(attn_1, proj_g1)
    qkv_p = product_left(full1_0, qkv_grad_0).astype(BF).reshape(rows, wr, 3 * wc)
    out_p = by_row(attn_0, proj_g0).astype(BF)
    parts = [qkv_p[:, :, :wc], qkv_p[:, :, wc : 2 * wc], qkv_p[:, :, 2 * wc :], out_p]
    first_pairs = [
        sum_pair(jnp.stack([parts[i], parts[2 + i]]).reshape(2, -1, wc), dps) for i in range(2)
    ]

    def column_sums(values):
        return jnp.sum(values, axis=0, dtype=F32)

    first = (row == 0).astype(F32)
    place = (lax.iota(jnp.int32, rows) == row).astype(F32)[:, None]
    qkv_s0 = column_sums(qkv_grad_0)
    qkv_s1 = column_sums(qkv_grad_t)
    vectors = jnp.concatenate(
        [
            column_sums(branch_g0),
            column_sums(proj_g0),
            column_sums(branch_g1) * first,
            (place * column_sums(proj_g1)[None]).reshape(-1),
            pre_s0[0],
            (place * pre_s1).reshape(-1),
            qkv_s0[:wc],
            qkv_s0[2 * wc :],
            qkv_s1[:wc],
            qkv_s1[2 * wc :],
        ]
    ).reshape(-1, wc)
    pad_rows = -vectors.shape[0] % 8
    qkv_grad_1, mixed1_g0, vectors, *sums = exchange(
        16,
        51,
        AllGatherRow(qkv_grad_t),
        ReduceScatterCol(product_right(qkv_grad_0, qkv_0).astype(BF), 4),
        AllGatherRow(jnp.pad(vectors, ((0, pad_rows), (0, 0)))),
        ReduceScatterCol(branch_p1, 2),
        first_pairs[0][0],
        first_pairs[1][0],
    )
    wide_1, sums = sums[0], sums[1:]
    first_ha = reduce_row(first_pairs[0][1](sums))
    first_hb = reduce_row(first_pairs[1][1](sums[1:]))
    qkv_g1 = product_left(full1_1, qkv_grad_1)
    image_grad = resid_g0 + norm_local_back(mixed1_g0 * (1.0 + mod_0[1]), norm1_0, inv1_0)
    branch_1, down_b0, mixed1_g1, text_b, vectors, image_grad = exchange(
        17,
        37,
        ReduceScatterRow(stack(wide_1.astype(BF), rows)),
        AllGatherDp(jnp.concatenate([down_ha, down_hb]), dps),
        ReduceScatterCol(product_right(qkv_grad_1, qkv_1).astype(BF)),
        AllGatherDp(text_h, dps),
        AllGatherDp(jnp.sum(vectors.reshape(rows, -1, wc), axis=0), dps),
        FromSequence(image_grad.astype(BF)),
    )
    vectors = jnp.sum(vectors.reshape(dps, -1, wc), axis=0).reshape(-1)
    branch_1 = branch_1 + down_b[1].astype(F32)
    text_out = (resid_1 + mod_1[5] * branch_1).astype(BF)[:TXT]
    norm1_g1 = mixed1_g1 * (1.0 + mod_1[1])

    sums_0 = jnp.stack(
        [
            jnp.sum(t, axis=0)
            for t in (
                mixed1_g0,
                mixed1_g0 * norm1_0,
                resid_g0 * proj_0,
                mixed2_g0,
                mixed2_g0 * norm2_0,
                cot0 * branch_0,
            )
        ]
    )
    sums_1 = jnp.stack(
        [
            jnp.sum(t, axis=0)
            for t in (
                mixed1_g1,
                mixed1_g1 * norm1_1,
                resid_g1 * proj_1,
                mixed2_g1,
                mixed2_g1 * norm2_1,
                cot1 * branch_1,
            )
        ]
    )
    up_b0, stats, cols_0, cols_1 = exchange(
        18,
        15,
        AllGatherDp(jnp.concatenate([up_ha, up_hb]), dps),
        AllGatherRow(row_stats(norm1_g1, norm1_g1 * norm1_1)),
        AllGatherCol(jnp.pad(sums_0, ((0, 2), (0, 0)))),
        AllGatherCol(jnp.pad(sums_1, ((0, 2), (0, 0)))),
    )
    image_grad = image_grad.astype(F32)
    text_grad = resid_g1 + norm_row_back(norm1_g1, norm1_1, inv1_1, stats)
    qkv_b1, rows_0 = exchange(
        19,
        19,
        AllGatherDp(qkv_g1.astype(BF), dps),
        AllGatherRow(jnp.sum(cols_0.reshape(cols, 8, rows * wr), axis=0)),
    )
    rows_0 = lax.dynamic_index_in_dim(
        rows_0.reshape(seqs, 8, rows, wr)[:, :6], row, 2, keepdims=False
    )
    mods_low = jnp.stack([rows_0, cols_1.reshape(seqs, 8, wr)[:, :6]]).astype(BF)
    mods_low = mods_low.reshape(2, seqs, 6 * wr)
    silu_part = product_right(mods_low[0], ada_w[0].reshape(wc, 6 * wr)) + product_right(
        mods_low[1], ada_w[1].reshape(wc, 6 * wr)
    )
    firsts, out_b1, mods_all, silu_all, silu_part = exchange(
        20,
        20,
        AllGatherDp(jnp.concatenate([first_ha, first_hb]), dps),
        AllGatherDp(out_g1.astype(BF), dps),
        AllGatherDp(mods_low.reshape(2 * seqs, 6 * wr).astype(F32), dps),
        AllGatherDp(jnp.pad(silu_low.astype(F32), ((0, 8 - seqs), (0, 0))), dps),
        AllGatherRow(jnp.pad(silu_part, ((0, 8 - seqs), (0, 0)))),
    )
    mods_all = mods_all.reshape(dps, 2, seqs, 6 * wr).transpose(1, 0, 2, 3)
    mods_all = mods_all.reshape(2, dps * seqs, 6 * wr).astype(BF)
    silu_all = silu_all.reshape(dps, 8, wc)[:, :seqs].reshape(dps * seqs, wc).astype(BF)
    ada_gw = jnp.stack(
        [product_left(silu_all, mods_all[s]).reshape(wc, 6, wr) for s in range(2)]
    )
    ada_gb = jnp.sum(mods_all, axis=1, dtype=F32).reshape(2, 6, wr)
    silu_sum = jnp.sum(silu_part.reshape(rows, 8, wc), axis=0)[:seqs]
    condition_grad = silu_slope(cond_value, silu_sum)
    row_sums = lax.dynamic_index_in_dim(
        vectors[: 4 * rows * wr].reshape(2, 2, rows, wr), row, 2, keepdims=False
    )
    rest = vectors[4 * rows * wr : 4 * rows * wr + 2 * wf + 4 * wc]
    up_gb = rest[: 2 * wf].reshape(2, wf)
    qkv_gb = rest[2 * wf :].reshape(2, 2, wc)

    up_g, down_g = finish(
        finish_feed_kernel, "finish_feed", [(2, wr, wf), (2, wf, wr)], up_b0, down_b0, text_b
    )
    qkv_g, out_g = finish(
        functools.partial(finish_rest_kernel, dps),
        "finish_rest",
        [(2, wr, 3 * wc), (2, wc, wr)],
        firsts,
        qkv_b1,
        out_b1,
    )

    return (
        image_out,
        text_out,
        image_grad,
        text_grad[:TXT],
        condition_grad,
        ada_gw,
        ada_gb,
        qkv_g.reshape(2, wr, 3, wc),
        qkv_gb,
        out_g,
        row_sums[:, 1],
        up_g,
        up_gb,
        down_g,
        row_sums[:, 0],
    )


def solution(mesh):
    placed = (
        P(("dp", "col"), "row"),
        P(("dp", "col"), "row"),
        P("dp", "col"),
        P(None, "col", None, "row"),
        P(None, None, "row"),
        P(None, "row", None, "col"),
        P(None, None, "col"),
        P(None, "col", "row"),
        P(None, "row"),
        P(None, "row", "col"),
        P(None, "col"),
        P(None, "col", "row"),
        P(None, "row"),
        P(("dp", "col"), "row"),
        P(("dp", "col"), "row"),
    )
    sizes = [mesh.shape[name] for name in ("dp", "row", "col")]
    return jax.shard_map(
        functools.partial(shards, *sizes),
        mesh=mesh,
        in_specs=placed,
        out_specs=(
            P(("dp", "col"), "row"),
            P(("dp", "col"), "row"),
            P(("dp", "col"), "row"),
            P(("dp", "col"), "row"),
            P("dp", "col"),
            P(None, "col", None, "row"),
            P(None, None, "row"),
            P(None, "row", None, "col"),
            P(None, None, "col"),
            P(None, "col", "row"),
            P(None, "row"),
            P(None, "row", "col"),
            P(None, "col"),
            P(None, "col", "row"),
            P(None, "row"),
        ),
        check_vma=False,
    )
```

```python
import functools

import jax
import jax.numpy as jnp
from jax import lax
from jax.experimental import pallas as pl
from jax.experimental.pallas import tpu as pltpu
from jax.sharding import PartitionSpec as P

D = 1536
HEAD = 64
IMG = 1024
TXT = 154
PAD = 160
SCALE = HEAD**-0.5
EPSILON = 1e-06
BF = jnp.bfloat16
F32 = jnp.float32


def product(left, right):
    return jnp.dot(left, right, preferred_element_type=F32)


def product_left(left, right):
    return lax.dot_general(left, right, (((0,), (0,)), ((), ())), preferred_element_type=F32)


def product_right(left, right):
    return lax.dot_general(left, right, (((1,), (1,)), ((), ())), preferred_element_type=F32)


def gelu_value(values):
    return jax.nn.gelu(values, approximate=True)


def gelu_slope(values, grad):
    return jax.vjp(gelu_value, values)[1](grad)[0]


def silu_slope(values, grad):
    return jax.vjp(jax.nn.silu, values)[1](grad)[0]


def gather(values, axis_name, axis=0):
    return lax.all_gather(values, axis_name, axis=axis, tiled=True)


def sum_pair(mine_first, dps):
    if dps == 2:
        return SumPair(mine_first.reshape(-1, mine_first.shape[2])), lambda values: values[0]
    total = lax.psum(mine_first, "dp")
    half = lax.dynamic_index_in_dim(total, lax.rem(lax.axis_index("dp"), 2), 0, False)
    return Body(lambda: None, [], []), lambda values: half


class Weight:
    def __init__(self, block, axis):
        self.block, self.axis = block, axis
        self.parity = lax.rem(lax.axis_index("dp"), 2)

    def cut(self, which):
        return lax.dynamic_slice_in_dim(self.block, which * 384, 384, self.axis)

    def gather(self, i, *earlier):
        mine = after(self.cut(2 * self.parity + i), *earlier)
        return lax.all_gather(mine, "row", tiled=True)

    def other(self, i):
        return self.cut(2 * (1 - self.parity) + i)

    def swap(self, i, gathered):
        return SwapBlocks(gathered, self.other(i))


def reduce_row(values):
    values = values.reshape(4, -1, values.shape[1])
    return lax.psum_scatter(values, "row", scatter_dimension=0)


def after(value, *others):
    return lax.optimization_barrier((value, others))[0]


def norm_local(values):
    mean = jnp.mean(values, axis=1, keepdims=True)
    square = jnp.mean(values * values, axis=1, keepdims=True)
    inverse = lax.rsqrt(square - mean * mean + EPSILON)
    return (values - mean) * inverse, inverse


def norm_local_back(grad, normed, inverse):
    total = jnp.mean(grad, axis=1, keepdims=True)
    cross = jnp.mean(grad * normed, axis=1, keepdims=True)
    return inverse * (grad - total - normed * cross)


def row_stats(first, second):
    pair = jnp.stack([jnp.sum(first, axis=1), jnp.sum(second, axis=1)])
    return jnp.pad(pair, ((0, 6), (0, 0)))


def row_means(stats):
    totals = jnp.sum(stats.reshape(4, 8, -1)[:, :2], axis=0) / D
    return totals[0][:, None], totals[1][:, None]


def norm_row(values, stats):
    mean, square = row_means(stats)
    inverse = lax.rsqrt(square - mean * mean + EPSILON)
    return (values - mean) * inverse, inverse


def norm_row_back(grad, normed, inverse, stats):
    total, cross = row_means(stats)
    return inverse * (grad - total - normed * cross)


def side(values, rows):
    width = values.shape[1]
    return values.reshape(rows, -1, width).transpose(1, 0, 2).reshape(-1, rows * width)


def stack(values, rows):
    count = values.shape[0]
    return values.reshape(count, rows, -1).transpose(1, 0, 2).reshape(rows * count, -1)


LOG2 = 1.4426950408889634


def dot_nt(left, right):
    return lax.dot_general(left, right, (((1,), (1,)), ((), ())), preferred_element_type=F32)


def dot_tn(left, right):
    return lax.dot_general(left, right, (((0,), (0,)), ((), ())), preferred_element_type=F32)


def head_mask(values, head):
    lane = lax.broadcasted_iota(jnp.int32, values.shape, 1)
    return jnp.where((lane >= head * HEAD) & (lane < (head + 1) * HEAD), values, 0)


def attend_body(pairs, full_i, full_t, oi, ot, li, lt, kim, vim, ktm, vtm):
    def pair(p, carry):
        at_q, at_k, at_v = (lanes((which * pairs + p) * 128, 128) for which in range(3))
        for h in range(2):
            kim[h] = head_mask(full_i[:, at_k], h)
            vim[h] = head_mask(full_i[:, at_v], h)
            ktm[h] = head_mask(full_t[:, at_k], h)
            vtm[h] = head_mask(full_t[:, at_v], h)

        def block(query):
            total = None
            rows = []
            for h in range(2):
                si = dot_nt(query, kim[h])
                st = dot_nt(query, ktm[h])
                lane = lax.broadcasted_iota(jnp.int32, st.shape, 1)
                st = jnp.where(lane < TXT, st, -1e30)
                peak = jnp.maximum(
                    jnp.max(si, axis=1, keepdims=True), jnp.max(st, axis=1, keepdims=True)
                )
                ei = jnp.exp2((si - peak) * (SCALE * LOG2))
                et = jnp.exp2((st - peak) * (SCALE * LOG2))
                norm = jnp.sum(ei, axis=1, keepdims=True) + jnp.sum(et, axis=1, keepdims=True)
                part = product(ei.astype(BF), vim[h]) + product(et.astype(BF), vtm[h])
                part = part / norm
                total = part if total is None else total + part
                rows.append(peak * (SCALE * LOG2) + jnp.log2(norm))
            lane = lax.broadcasted_iota(jnp.int32, total.shape, 1)
            stats = jnp.where(lane == 0, rows[0], jnp.where(lane == 1, rows[1], 0.0))
            return total.astype(BF), jnp.transpose(stats)[:8]

        for b in range(IMG // 256):
            at = pl.ds(b * 256, 256)
            oi[at, at_q], li[p, :, at] = block(full_i[at, at_q])
        ot[:, at_q], lt[p] = block(full_t[:, at_q])
        return carry

    lax.fori_loop(0, pairs, pair, 0)


def attend(qkv_i, qkv_t):
    width = qkv_i.shape[1] // 3
    pairs = width // 128
    return Body(
        functools.partial(attend_body, pairs),
        [qkv_i, qkv_t],
        [
            jax.ShapeDtypeStruct((IMG, width), BF),
            jax.ShapeDtypeStruct((PAD, width), BF),
            jax.ShapeDtypeStruct((pairs, 8, IMG), F32),
            jax.ShapeDtypeStruct((pairs, 8, PAD), F32),
        ],
        [pltpu.VMEM((2, n, 128), BF) for n in (IMG, IMG, PAD, PAD)],
    )


def attend_back_body(
    pairs, full_i, full_t, oi, ot, gi, gt, li, lt, di, dt, aki, avi, akt, avt
):
    lane8 = lax.broadcasted_iota(jnp.int32, (8, 128), 1) // HEAD
    row8 = lax.broadcasted_iota(jnp.int32, (8, 128), 0)
    pick = (lane8 == row8).astype(F32)

    def pair(p, carry):
        at_q, at_k, at_v = (lanes((which * pairs + p) * 128, 128) for which in range(3))
        for acc in (aki, avi, akt, avt):
            acc[...] = jnp.zeros_like(acc)

        def block(query, out, grad, logsum):
            products = grad.astype(F32) * out.astype(F32)
            delta = lax.dot_general(
                pick, products, (((1,), (1,)), ((), ())),
                preferred_element_type=F32, precision=lax.Precision.HIGHEST,
            )
            total = None
            for h in range(2):
                qm = head_mask(query, h)
                gm = head_mask(grad, h)
                part = None
                for full, ak, av, text in ((full_i, aki, avi, False), (full_t, akt, avt, True)):
                    keys, values = full[:, at_k], full[:, at_v]
                    scores = dot_nt(keys, qm) * (SCALE * LOG2) - logsum[h : h + 1]
                    prob = jnp.exp2(scores)
                    if text:
                        place = lax.broadcasted_iota(jnp.int32, prob.shape, 0)
                        prob = jnp.where(place < TXT, prob, 0.0)
                    grads = (prob * (dot_nt(values, gm) - delta[h : h + 1])).astype(BF)
                    av[...] += product(prob.astype(BF), gm)
                    ak[...] += product(grads, qm)
                    term = dot_tn(grads, keys)
                    part = term if part is None else part + term
                part = head_mask(part, h)
                total = part if total is None else total + part
            return (total * SCALE).astype(BF)

        for b in range(IMG // 256):
            at = pl.ds(b * 256, 256)
            di[at, at_q] = block(full_i[at, at_q], oi[at, at_q], gi[at, at_q], li[p, :, at])
        dt[:, at_q] = block(full_t[:, at_q], ot[:, at_q], gt[:, at_q], lt[p])
        di[:, at_k] = (aki[...] * SCALE).astype(BF)
        di[:, at_v] = avi[...].astype(BF)
        dt[:, at_k] = (akt[...] * SCALE).astype(BF)
        dt[:, at_v] = avt[...].astype(BF)
        return carry

    lax.fori_loop(0, pairs, pair, 0)


def attend_back(qkv_i, qkv_t, out_i, out_t, grad_i, grad_t, log_i, log_t):
    pairs = qkv_i.shape[1] // 384
    return Body(
        functools.partial(attend_back_body, pairs),
        [qkv_i, qkv_t, out_i, out_t, grad_i, grad_t, log_i, log_t],
        [jax.ShapeDtypeStruct(v.shape, BF) for v in (qkv_i, qkv_t)],
        [pltpu.VMEM((n, 128), F32) for n in (IMG, IMG, PAD, PAD)],
    )


MESH = pl.DeviceIdType.MESH


def lanes(start, size):
    return pl.ds(pl.multiple_of(start, 128), size)


def cost(micros):
    return pl.CostEstimate(flops=0, bytes_accessed=micros * 3_500_000, transcendentals=0)


def span(start, size):
    unit = 16 if size % 16 == 0 else 8
    return pl.ds(pl.multiple_of(start, unit), size)


class AllGatherCol:
    def __init__(self, value, pieces=1):
        self.ins = [value]
        n, w = value.shape
        self.n, self.pieces, self.step = n, pieces, n // pieces
        self.outs = [jax.ShapeDtypeStruct((4 * n, w), value.dtype)]
        self.scratch = [pltpu.SemaphoreType.DMA((3 * pieces,)) for _ in range(2)]

    def peers(self, me):
        return [(me[0], me[1], me[2] ^ 1), (me[0], me[1], me[2] ^ 2)]

    greets = awaits = peers

    def move(self, refs, me, which, i):
        (value,), (out,), (send, recv) = refs
        core, across = self.peers(me)
        owner = me[2] ^ 2 if which == 2 else me[2]
        slot = out.at[span(owner * self.n + i * self.step, self.step)]
        source = slot if which == 2 else value.at[pl.ds(i * self.step, self.step)]
        k = which * self.pieces + i
        return pltpu.make_async_remote_copy(
            source, slot, send.at[k], recv.at[k],
            device_id=across if which == 0 else core, device_id_type=MESH,
        )

    def start(self, refs, me):
        for which in range(2):
            for i in range(self.pieces):
                self.move(refs, me, which, i).start()
        (value,), (out,), _ = refs
        out[span(me[2] * self.n, self.n)] = value[...]

    def middle(self, refs, me):
        for i in range(self.pieces):
            self.move(refs, me, 0, i).wait_recv()
            self.move(refs, me, 2, i).start()

    def wait_core(self, refs, me):
        for i in range(self.pieces):
            self.move(refs, me, 1, i).wait_recv()

    def finish(self, refs, me, core=True):
        if core:
            self.wait_core(refs, me)
        for which in range(3):
            for i in range(self.pieces):
                move = self.move(refs, me, which, i)
                move.wait_send()
                if which == 2:
                    move.wait_recv()


class ReduceScatterCol:
    def __init__(self, value, pieces=1):
        self.ins = [value]
        n, w = value.shape[0] // 4, value.shape[1]
        self.n, self.pieces, self.step = n, pieces, n // pieces
        self.outs = [jax.ShapeDtypeStruct((n, w), F32)]
        self.scratch = [pltpu.VMEM((n, w), BF) for _ in range(4)]
        self.scratch += [pltpu.SemaphoreType.DMA((3 * pieces,)) for _ in range(2)]

    peers = AllGatherCol.peers
    greets = awaits = peers

    def move(self, refs, me, which, i):
        (part,), _, (first, second, third, total, send, recv) = refs
        core, across = self.peers(me)
        at = pl.ds(i * self.step, self.step)
        if which == 2:
            source, target = total.at[at], third.at[at]
        else:
            owner = me[2] ^ 3 if which == 0 else me[2] ^ 1
            source = part.at[span(owner * self.n + i * self.step, self.step)]
            target = (first, second)[which].at[at]
        k = which * self.pieces + i
        return pltpu.make_async_remote_copy(
            source, target, send.at[k], recv.at[k],
            device_id=across if which == 2 else core, device_id_type=MESH,
        )

    def start(self, refs, me):
        for which in range(2):
            for i in range(self.pieces):
                self.move(refs, me, which, i).start()

    def middle(self, refs, me):
        (part,), _, (first, second, third, total, send, recv) = refs
        for i in range(self.pieces):
            self.move(refs, me, 0, i).wait_recv()
            at = pl.ds(i * self.step, self.step)
            mine = part[span((me[2] ^ 2) * self.n + i * self.step, self.step)]
            total[at] = (mine.astype(F32) + first[at].astype(F32)).astype(BF)
            self.move(refs, me, 2, i).start()

    def finish(self, refs, me):
        (part,), (out,), (first, second, third, total, send, recv) = refs
        for i in range(self.pieces):
            for which in (1, 2):
                self.move(refs, me, which, i).wait_recv()
            at = pl.ds(i * self.step, self.step)
            mine = part[span(me[2] * self.n + i * self.step, self.step)].astype(F32)
            out[at] = mine + second[at].astype(F32) + third[at].astype(F32)
        for which in range(3):
            for i in range(self.pieces):
                self.move(refs, me, which, i).wait_send()


class AllGatherRow:
    axis = 1

    def __init__(self, value, size=4):
        self.ins = [value]
        n, w = value.shape
        self.n, self.size = n, size
        self.outs = [jax.ShapeDtypeStruct((size * n, w), value.dtype)]
        self.scratch = [pltpu.SemaphoreType.DMA((size - 1,)) for _ in range(2)]

    def peers(self, me):
        found = []
        for k in range(1, self.size):
            device = list(me)
            device[self.axis] = lax.rem(me[self.axis] + k, self.size)
            found.append(tuple(device))
        return found

    greets = awaits = peers

    def move(self, refs, me, k):
        (value,), (out,), (send, recv) = refs
        return pltpu.make_async_remote_copy(
            value, out.at[span(me[self.axis] * self.n, self.n)], send.at[k], recv.at[k],
            device_id=self.peers(me)[k], device_id_type=MESH,
        )

    def start(self, refs, me):
        for k in range(self.size - 1):
            self.move(refs, me, k).start()
        (value,), (out,), _ = refs
        out[span(me[self.axis] * self.n, self.n)] = value[...]

    def middle(self, refs, me):
        pass

    def finish(self, refs, me):
        for k in range(self.size - 1):
            self.move(refs, me, k).wait()


class AllGatherDp(AllGatherRow):
    axis = 0


class AllToAllRow(AllGatherRow):
    def __init__(self, value):
        self.ins = [value]
        self.n, self.size = value.shape[0] // 4, 4
        self.outs = [jax.ShapeDtypeStruct(value.shape, value.dtype)]
        self.scratch = [pltpu.SemaphoreType.DMA((3,)) for _ in range(2)]

    def move(self, refs, me, k):
        (value,), (out,), (send, recv) = refs
        target = self.peers(me)[k]
        return pltpu.make_async_remote_copy(
            value.at[span(target[1] * self.n, self.n)],
            out.at[span(me[1] * self.n, self.n)],
            send.at[k], recv.at[k],
            device_id=target, device_id_type=MESH,
        )

    def start(self, refs, me):
        for k in range(3):
            self.move(refs, me, k).start()
        (value,), (out,), _ = refs
        at = span(me[1] * self.n, self.n)
        out[at] = value[at]


class SwapBlocks:
    def __init__(self, value, own):
        self.ins = [value, own]
        self.n = own.shape[0]
        self.outs = [jax.ShapeDtypeStruct((2 * value.shape[0], value.shape[1]), value.dtype)]
        self.scratch = [pltpu.SemaphoreType.DMA((3,)) for _ in range(2)]

    def peers(self, me):
        return [(me[0] ^ 1, me[1], me[2])]

    greets = awaits = peers

    def move(self, refs, me, k):
        (value, own), (out,), (send, recv) = refs
        block = lax.rem(me[1] + k + 1, 4)
        place = (lax.rem(me[0], 2) * 4 + block) * self.n
        return pltpu.make_async_remote_copy(
            value.at[span(block * self.n, self.n)], out.at[span(place, self.n)],
            send.at[k], recv.at[k],
            device_id=self.peers(me)[0], device_id_type=MESH,
        )

    def start(self, refs, me):
        for k in range(3):
            self.move(refs, me, k).start()
        (value, own), (out,), _ = refs
        parity = lax.rem(me[0], 2)
        out[span(parity * 4 * self.n, 4 * self.n)] = value[...]
        out[span(((1 - parity) * 4 + me[1]) * self.n, self.n)] = own[...]

    def middle(self, refs, me):
        pass

    def finish(self, refs, me):
        for k in range(3):
            self.move(refs, me, k).wait()


class SumPair:
    def __init__(self, value):
        self.ins = [value]
        n, w = value.shape[0] // 2, value.shape[1]
        self.n = n
        self.outs = [jax.ShapeDtypeStruct((n, w), BF)]
        self.scratch = [pltpu.VMEM((n, w), BF)]
        self.scratch += [pltpu.SemaphoreType.DMA((1,)) for _ in range(2)]

    def peers(self, me):
        return [(1 - me[0], me[1], me[2])]

    greets = awaits = peers

    def move(self, refs, me):
        (part,), _, (held, send, recv) = refs
        return pltpu.make_async_remote_copy(
            part.at[span((1 - me[0]) * self.n, self.n)], held, send.at[0], recv.at[0],
            device_id=self.peers(me)[0], device_id_type=MESH,
        )

    def start(self, refs, me):
        self.move(refs, me).start()

    def middle(self, refs, me):
        pass

    def finish(self, refs, me):
        (part,), (out,), (held, send, recv) = refs
        self.move(refs, me).wait()
        mine = part[span(me[0] * self.n, self.n)].astype(F32)
        out[...] = (mine + held[...].astype(F32)).astype(BF)


class ReduceScatterRow:
    def __init__(self, value):
        self.ins = [value]
        n, w = value.shape[0] // 4, value.shape[1]
        self.n = n
        self.outs = [jax.ShapeDtypeStruct((n, w), F32)]
        self.scratch = [pltpu.VMEM((3, n, w), BF)]
        self.scratch += [pltpu.SemaphoreType.DMA((3,)) for _ in range(2)]

    axis, size = 1, 4
    peers = AllGatherRow.peers
    greets = awaits = peers

    def move(self, refs, me, k):
        (part,), _, (held, send, recv) = refs
        target = self.peers(me)[k]
        return pltpu.make_async_remote_copy(
            part.at[span(target[1] * self.n, self.n)], held.at[k], send.at[k], recv.at[k],
            device_id=target, device_id_type=MESH,
        )

    def start(self, refs, me):
        for k in (1, 0, 2):
            self.move(refs, me, k).start()

    def middle(self, refs, me):
        pass

    def finish(self, refs, me):
        (part,), (out,), (held, send, recv) = refs
        for k in range(3):
            self.move(refs, me, k).wait()
        total = part[span(me[1] * self.n, self.n)].astype(F32)
        for k in range(3):
            total = total + held[k].astype(F32)
        out[...] = total


class ToSequence:
    def __init__(self, value):
        self.ins = [value]
        self.n, self.w = value.shape[0] // 4, value.shape[1]
        self.outs = [jax.ShapeDtypeStruct((self.n, 4 * self.w), value.dtype)]
        self.scratch = [pltpu.SemaphoreType.DMA((4,)) for _ in range(2)]

    def targets(self, me):
        return [(me[0], me[2], k) for k in range(4)]

    def sources(self, me):
        return [(me[0], k, me[1]) for k in range(4)]

    def greets(self, me):
        return [
            (device, jnp.logical_not((device[1] == me[1]) & (device[2] == me[2])))
            for device in self.sources(me)
        ]

    def awaits(self, me):
        return self.targets(me)

    def remote(self, me, device):
        return jnp.logical_not((device[1] == me[1]) & (device[2] == me[2]))

    def place(self, refs, me, k):
        (value,), (out,), _ = refs
        source = value.at[pl.ds(k * self.n, self.n)]
        return source, out.at[:, pl.ds(pl.multiple_of(me[1] * self.w, 128), self.w)]

    def outgoing(self, refs, me, k):
        send, recv = refs[2]
        source, target = self.place(refs, me, k)
        return pltpu.make_async_remote_copy(
            source, target, send.at[k], recv.at[me[1]],
            device_id=self.targets(me)[k], device_id_type=MESH,
        )

    def incoming(self, refs, me, k):
        send, recv = refs[2]
        (value,), (out,), _ = refs
        landing = out.at[:, pl.ds(k * self.w, self.w)]
        return pltpu.make_async_remote_copy(
            value.at[pl.ds(0, self.n)], landing, send.at[k], recv.at[k],
            device_id=self.targets(me)[k], device_id_type=MESH,
        )

    def copy_own(self, refs, me):
        (value,), (out,), _ = refs
        at = pl.ds(pl.multiple_of(me[1] * self.w, 128), self.w)
        out[:, at] = value[span(me[2] * self.n, self.n)]

    def start(self, refs, me):
        for k in range(4):
            @pl.when(self.remote(me, self.targets(me)[k]))
            def _():
                self.outgoing(refs, me, k).start()

        @pl.when(me[1] == me[2])
        def _():
            self.copy_own(refs, me)

    def middle(self, refs, me):
        pass

    def finish(self, refs, me):
        for k in range(4):
            @pl.when(self.remote(me, self.targets(me)[k]))
            def _():
                self.outgoing(refs, me, k).wait_send()

            @pl.when(self.remote(me, self.sources(me)[k]))
            def _():
                self.incoming(refs, me, k).wait_recv()


class FromSequence(ToSequence):
    def __init__(self, value):
        self.ins = [value]
        self.n, self.w = value.shape[0], value.shape[1] // 4
        self.outs = [jax.ShapeDtypeStruct((4 * self.n, self.w), value.dtype)]
        self.scratch = [pltpu.SemaphoreType.DMA((4,)) for _ in range(2)]

    def targets(self, me):
        return [(me[0], k, me[1]) for k in range(4)]

    def sources(self, me):
        return [(me[0], me[2], k) for k in range(4)]

    def outgoing(self, refs, me, k):
        (value,), (out,), (send, recv) = refs
        return pltpu.make_async_remote_copy(
            value.at[:, pl.ds(k * self.w, self.w)],
            out.at[span(me[2] * self.n, self.n)],
            send.at[k], recv.at[me[2]],
            device_id=self.targets(me)[k], device_id_type=MESH,
        )

    def incoming(self, refs, me, k):
        (value,), (out,), (send, recv) = refs
        return pltpu.make_async_remote_copy(
            value.at[:, pl.ds(0, self.w)],
            out.at[pl.ds(k * self.n, self.n)],
            send.at[k], recv.at[k],
            device_id=self.targets(me)[k], device_id_type=MESH,
        )

    def copy_own(self, refs, me):
        (value,), (out,), _ = refs
        at = pl.ds(pl.multiple_of(me[1] * self.w, 128), self.w)
        out[span(me[2] * self.n, self.n)] = value[:, at]


class Body:
    def __init__(self, work, ins, outs, scratch=()):
        self.work, self.ins, self.outs, self.scratch = work, list(ins), list(outs), list(scratch)


def exchange_kernel(ops, *refs):
    me = tuple(lax.axis_index(name) for name in ("dp", "row", "col"))
    refs = list(refs)
    parts = []
    for kind in ("ins", "outs", "scratch"):
        taken = []
        for op in ops:
            count = len(getattr(op, kind))
            taken.append(refs[:count])
            refs = refs[count:]
        parts.append(taken)
    parts = list(zip(*parts))
    moving = [(op, part) for op, part in zip(ops, parts) if not isinstance(op, Body)]
    barrier = pltpu.get_barrier_semaphore()
    count = 0
    for op, _ in moving:
        for item in op.greets(me):
            device, wanted = item if len(item) == 2 else (item, None)
            if wanted is None:
                pl.semaphore_signal(barrier, 1, device_id=device, device_id_type=MESH)
            else:
                @pl.when(wanted)
                def _():
                    pl.semaphore_signal(barrier, 1, device_id=device, device_id_type=MESH)
        if isinstance(op, ToSequence):
            count = count + 4 - (me[1] == me[2]).astype(jnp.int32)
        else:
            count = count + len(op.awaits(me))
    pl.semaphore_wait(barrier, count)
    for op, part in moving:
        op.start(part, me)
    for op, part in zip(ops, parts):
        if isinstance(op, Body):
            op.work(*part[0], *part[1], *part[2])
    for op, part in moving:
        op.middle(part, me)
    for op, part in moving:
        op.finish(part, me)


def exchange(number, micros, *ops, name="exchange"):
    ins = [value for op in ops for value in op.ins]
    outs = [shape for op in ops for shape in op.outs]
    results = pl.pallas_call(
        functools.partial(exchange_kernel, ops),
        in_specs=[pl.BlockSpec(memory_space=pltpu.VMEM)] * len(ins),
        out_specs=[pl.BlockSpec(memory_space=pltpu.VMEM)] * len(outs),
        out_shape=outs,
        scratch_shapes=[shape for op in ops for shape in op.scratch],
        compiler_params=pltpu.CompilerParams(
            collective_id=number, has_side_effects=True, vmem_limit_bytes=60 * 1024 * 1024
        ),
        cost_estimate=cost(micros),
        name=name + str(number),
    )(*ins)
    return results


def gelu_pair(values):
    inner = 0.7978845608028654 * (values + 0.044715 * values * values * values)
    bend = jnp.tanh(inner)
    half = 0.5 * (1.0 + bend)
    slope = half + values * (0.5 * (1.0 - bend * bend)) * (
        0.7978845608028654 * (1.0 + 0.134145 * values * values)
    )
    return values * half, slope


def block_copies(target, parts, sems, first, by_rows):
    copies = []
    for i, part in enumerate(parts):
        for k in range(2):
            for r in range(4):
                source = part.at[pl.ds((k * 4 + r) * 384, 384)]
                along, cross = pl.ds(r * 384, 384), pl.ds((2 * k + i) * 384, 384)
                place = target.at[cross, along] if by_rows else target.at[along, cross]
                copies.append(pltpu.make_async_copy(source, place, sems.at[first]))
                first += 1
    return copies


def input_kernel(x, part_a, part_b, bias, qkv, qkv_w, out_w, weight, sems):
    copies = block_copies(weight, (part_a, part_b), sems, 0, False)
    for copy in copies:
        copy.start()
    for copy in copies:
        copy.wait()
    width = qkv.shape[1]
    back = [pltpu.make_async_copy(weight.at[:, pl.ds(0, width)], qkv_w, sems.at[0])]
    for r in range(4):
        back.append(
            pltpu.make_async_copy(
                weight.at[pl.ds(r * 384, 384), pl.ds(width, 384)],
                out_w.at[:, pl.ds(r * 384, 384)],
                sems.at[1 + r],
            )
        )
    for copy in back:
        copy.start()

    def step(i, _):
        at = lanes(i * 384, 384)
        qkv[:, at] = (product(x[...], weight[:, at]) + bias[:, at]).astype(BF)
        return _

    lax.fori_loop(0, width // 384, step, 0)
    for copy in back:
        copy.wait()


def input_product(x, parts, bias):
    rows, depth = x.shape
    width = 3 * 384
    return pl.pallas_call(
        input_kernel,
        in_specs=[
            pl.BlockSpec(memory_space=pltpu.VMEM),
            *[pl.BlockSpec(memory_space=pl.ANY)] * 2,
            pl.BlockSpec(memory_space=pltpu.VMEM),
        ],
        out_specs=[
            pl.BlockSpec(memory_space=pltpu.VMEM),
            pl.BlockSpec(memory_space=pl.ANY),
            pl.BlockSpec(memory_space=pl.ANY),
        ],
        out_shape=[
            jax.ShapeDtypeStruct((rows, width), BF),
            jax.ShapeDtypeStruct((depth, width), BF),
            jax.ShapeDtypeStruct((384, depth), BF),
        ],
        scratch_shapes=[pltpu.VMEM((depth, 1536), BF), pltpu.SemaphoreType.DMA((16,))],
        compiler_params=pltpu.CompilerParams(vmem_limit_bytes=56 * 1024 * 1024),
        cost_estimate=cost(8),
        name="input_product",
    )(x, *parts, bias)


def feed_kernel(ops, me, refs):
    gather_0, sums_t, gather_r, gather_t, scatter_0, scatter_t, scatter_b, swap = ops
    ins, outs, scratch = refs
    (mixed_0, resid_t, mod_t, grad_0, grad_t, bias_0, bias_t) = ins[:7]
    (down_b, own_b, down_a, up_a, up_b, text_p) = ins[7:]
    (mixed_g0, wide_g1, stats_out, sum_0, sum_t, branch_0) = outs[:6]
    (gup, gdown, gtext, branch_t) = outs[6:]
    (full_0, up, down, hidden, pre_g, part_0, stage, text_w) = scratch[:8]
    (stats_in, mixed_t, wide_t, side_t, full_t, hidden_t, pre_gt, part_t) = scratch[8:16]
    (w_sems, s_sems, part_b, down_all) = scratch[16:20]
    rest = scratch[20:]
    dp, row, col = me
    refs_g0 = ((mixed_0,), (full_0,), rest[0:2])
    refs_st = ((stats_in,), (stats_out,), rest[2:4])
    refs_gr = ((mixed_t,), (wide_t,), rest[4:6])
    refs_gt = ((side_t,), (full_t,), rest[6:8])
    refs_s0 = ((part_0,), (mixed_g0,), rest[8:14])
    refs_s1 = ((part_t,), (wide_g1,), rest[14:20])
    refs_sb = ((part_b,), (branch_0,), rest[20:26])
    refs_sd = ((down_b, own_b), (down_all,), rest[26:28])

    swap.start(refs_sd, me)
    copies = block_copies(up, (up_a, up_b), w_sems, 0, False)
    copies += block_copies(down, (down_a,), w_sems, 16, True)
    parity = lax.rem(dp, 2)
    for k in range(2):
        for r in range(4):
            for w in range(2):
                at = text_w.at[w, pl.ds(k * 192, 192), pl.ds(r * 384, 384)]
                source = text_p.at[pl.ds((k * 4 + r) * 384 + w * 192, 192)]
                copies.append(pltpu.make_async_copy(source, at, w_sems.at[24 + 8 * k + 2 * r + w]))
    for copy in copies:
        copy.start()
    gather_0.start(refs_g0, me)

    resid = resid_t[...]
    lane = lax.broadcasted_iota(jnp.int32, (PAD, 128), 1)
    pair = jnp.where(
        lane == 0,
        jnp.sum(resid, axis=1, keepdims=True),
        jnp.where(lane == 1, jnp.sum(resid * resid, axis=1, keepdims=True), 0.0),
    )
    stats_in[...] = jnp.transpose(pair)[:8]
    sums_t.start(refs_st, me)
    sums_t.finish(refs_st, me)
    total = stats_out[0:8] + stats_out[8:16] + stats_out[16:24] + stats_out[24:32]
    total = jnp.transpose(jnp.concatenate([total, jnp.zeros((120, PAD), F32)], axis=0)) / D
    mean, square = total[:, 0:1], total[:, 1:2]
    normed = (resid - mean) * lax.rsqrt(square - mean * mean + EPSILON)
    mixed_t[...] = (normed * mod_t[1:2] + mod_t[0:1]).astype(BF)
    gather_r.start(refs_gr, me)
    for copy in copies:
        copy.wait()
    swap.finish(refs_sd, me)
    for k in range(2):
        for r in range(4):
            place = down.at[pl.ds((2 * k + 1) * 384, 384), pl.ds(r * 384, 384)]
            place[...] = down_all[pl.ds((k * 4 + r) * 384, 384), :]
    sum_0[...] = jnp.zeros_like(sum_0)
    sum_t[...] = jnp.zeros_like(sum_t)

    def quarter(i, carry):
        @pl.when(i == 2)
        def _():
            gather_r.finish(refs_gr, me)
            for r in range(4):
                side_t[:, pl.ds(r * 384, 384)] = wide_t[pl.ds(r * PAD, PAD), :]
            gather_0.middle(refs_g0, me)
            gather_0.finish(refs_g0, me, False)
            gather_t.start(refs_gt, me)

        @pl.when(i == 1)
        def _():
            gather_0.wait_core(refs_g0, me)

        at = span((col ^ (i ^ (i // 2))) * 256, 256)

        def tile(j, carry):
            cut = lanes(j * 512, 512)
            pre = product(full_0[at, :], up[:, cut]) + bias_0[:, cut]
            value, slope = gelu_pair(pre)
            hidden[at, cut] = value.astype(BF)
            back = product_right(grad_0[at, :], down[cut, :])
            grad = (back * slope).astype(BF)
            pre_g[at, cut] = grad
            sum_0[:, cut] += jnp.sum(grad.astype(F32), axis=0, keepdims=True)
            return carry

        lax.fori_loop(0, 3, tile, 0)

        def tile_back(j, carry):
            cut = lanes(j * 512, 512)
            part_0[at, cut] = product_right(pre_g[at, :], up[cut, :]).astype(BF)
            return carry

        lax.fori_loop(0, 3, tile_back, 0)
        return carry

    lax.fori_loop(0, 4, quarter, 0)
    scatter_0.start(refs_s0, me)
    scatter_0.middle(refs_s0, me)
    gather_t.middle(refs_gt, me)
    gather_t.finish(refs_gt, me)

    def text_quarter(i, carry):
        at = span(i * PAD, PAD)
        pre = product_right(full_t[at, :], text_w[0]) + bias_t[...]
        value, slope = gelu_pair(pre)
        hidden_t[at, :] = value.astype(BF)
        grad = (product_right(grad_t[at, :], text_w[1]) * slope).astype(BF)
        pre_gt[at, :] = grad
        sum_t[...] += jnp.sum(grad.astype(F32), axis=0, keepdims=True)
        part_t[at, :] = product(grad, text_w[0]).astype(BF)
        return carry

    lax.fori_loop(0, 4, text_quarter, 0)
    scatter_t.start(refs_s1, me)
    scatter_t.middle(refs_s1, me)

    def branch_quarter(i, carry):
        at = span(i * 256, 256)
        for j in range(3):
            cut = pl.ds(j * 512, 512)
            part_b[at, cut] = product(hidden[at, :], down[:, cut]).astype(BF)
        return carry

    lax.fori_loop(0, 4, branch_quarter, 0)
    scatter_b.start(refs_sb, me)
    scatter_b.middle(refs_sb, me)

    def put(slot, moves):
        for k, (source, target) in enumerate(moves):
            pltpu.make_async_copy(source, target, s_sems.at[slot, k]).start()

    def done(slot, moves):
        for k, (source, target) in enumerate(moves):
            pltpu.make_async_copy(source, target, s_sems.at[slot, k]).wait()

    def staged(count, value_of, moves_of):
        def step(i, carry):
            slot = lax.rem(i, 2)

            @pl.when(i >= 2)
            def _():
                done(slot, moves_of(i - 2, stage.at[slot]))

            value_of(i, stage.at[slot])
            put(slot, moves_of(i, stage.at[slot]))
            return carry

        lax.fori_loop(0, count, step, 0)
        for i in (count - 2, count - 1):
            done(i % 2, moves_of(i, stage.at[i % 2]))

    def value_of(i, place):
        cut = lanes(i * 384, 384)
        for j in range(3):
            at = pl.ds(j * 512, 512)
            place[:, at] = product_left(hidden[:, cut], grad_0[:, at]).astype(BF)

    def moves_of(i, place):
        return [
            (
                place.at[:, pl.ds(r * 384, 384)],
                gdown.at[lax.rem(i, 2), i // 2, r],
            )
            for r in range(4)
        ]

    staged(4, value_of, moves_of)

    def value_of(i, place):
        for j in range(3):
            at = pl.ds(j * 512, 512)
            left = full_0[:, lanes(i * 384, 384)]
            place[:, at] = product_left(left, pre_g[:, at]).astype(BF)

    def moves_of(i, place):
        return [
            (place.at[:, pl.ds((2 * k + q) * 384, 384)], gup.at[q, k, i])
            for k in range(2)
            for q in range(2)
        ]

    staged(4, value_of, moves_of)

    def value_of(i, place):
        @pl.when(i == 0)
        def _():
            for j in range(3):
                at = pl.ds(j * 512, 512)
                place[:, at] = product_left(pre_gt[...], full_t[:, at]).astype(BF)

        @pl.when(i == 1)
        def _():
            for j in range(3):
                at = pl.ds(j * 512, 512)
                place[:, at] = product_left(hidden_t[...], grad_t[:, at]).astype(BF)

    def moves_of(i, place):
        return [
            (place.at[pl.ds(k * 192, 192)], gtext.at[i, k]) for k in range(2)
        ]

    staged(2, value_of, moves_of)

    def value_of(i, place):
        at = span(i * PAD, PAD)
        place[pl.ds(0, PAD)] = product(hidden_t[at, :], text_w[1]).astype(BF)

    def moves_of(i, place):
        return [(place.at[pl.ds(0, PAD)], branch_t.at[span(i * PAD, PAD)])]

    staged(4, value_of, moves_of)
    scatter_0.finish(refs_s0, me)
    scatter_t.finish(refs_s1, me)
    scatter_b.finish(refs_sb, me)


def feed(number, mixed_0, resid_t, mod_t, grad_0, grad_t, bias_0, bias_t, *weights):
    def shape(*dims, dtype=BF):
        return jax.ShapeDtypeStruct(dims, dtype)

    ops = (
        AllGatherCol(mixed_0, 4),
        AllGatherRow(shape(8, PAD, dtype=F32)),
        AllGatherRow(shape(PAD, 384)),
        AllGatherCol(shape(PAD, 1536), 2),
        ReduceScatterCol(shape(1024, 1536), 4),
        ReduceScatterCol(shape(640, 1536), 2),
        ReduceScatterCol(shape(1024, 1536), 4),
        SwapBlocks(weights[0], weights[1]),
    )

    def kernel(*refs):
        me = tuple(lax.axis_index(name) for name in ("dp", "row", "col"))
        barrier = pltpu.get_barrier_semaphore()
        peers = ops[0].peers(me) + ops[1].peers(me) + ops[-1].peers(me)
        for device in peers:
            pl.semaphore_signal(barrier, 1, device_id=device, device_id_type=MESH)
        pl.semaphore_wait(barrier, len(peers))
        feed_kernel(ops, me, (refs[:13], refs[13:23], refs[23:]))

    outs = [
        shape(256, 1536, dtype=F32),
        shape(PAD, 1536, dtype=F32),
        shape(32, PAD, dtype=F32),
        shape(1, 1536, dtype=F32),
        shape(1, 384, dtype=F32),
        shape(256, 1536, dtype=F32),
        shape(2, 2, 4, 384, 384),
        shape(2, 2, 4, 384, 384),
        shape(2, 2, 192, 1536),
        shape(640, 1536),
    ]
    vmem, hbm = pl.BlockSpec(memory_space=pltpu.VMEM), pl.BlockSpec(memory_space=pl.ANY)
    return pl.pallas_call(
        kernel,
        in_specs=[vmem] * 9 + [hbm] * 4,
        out_specs=[vmem] * 6 + [hbm] * 4,
        out_shape=outs,
        scratch_shapes=[
            pltpu.VMEM((1024, 1536), BF),
            pltpu.VMEM((1536, 1536), BF),
            pltpu.VMEM((1536, 1536), BF),
            pltpu.VMEM((1024, 1536), BF),
            pltpu.VMEM((1024, 1536), BF),
            pltpu.VMEM((1024, 1536), BF),
            pltpu.VMEM((2, 384, 1536), BF),
            pltpu.VMEM((2, 384, 1536), BF),
            pltpu.VMEM((8, PAD), F32),
            pltpu.VMEM((PAD, 384), BF),
            pltpu.VMEM((640, 384), BF),
            pltpu.VMEM((PAD, 1536), BF),
            pltpu.VMEM((640, 1536), BF),
            pltpu.VMEM((640, 384), BF),
            pltpu.VMEM((640, 384), BF),
            pltpu.VMEM((640, 1536), BF),
            pltpu.SemaphoreType.DMA((40,)),
            pltpu.SemaphoreType.DMA((2, 4)),
            pltpu.VMEM((1024, 1536), BF),
            pltpu.VMEM((3072, 384), BF),
        ]
        + [item for op in ops for item in op.scratch],
        compiler_params=pltpu.CompilerParams(
            collective_id=number, has_side_effects=True, vmem_limit_bytes=62 * 1024 * 1024
        ),
        cost_estimate=cost(90),
        name="feed",
    )(mixed_0, resid_t, mod_t, grad_0, grad_t, bias_0, bias_t, *weights)


class SumPairFar(SumPair):
    def __init__(self, value):
        super().__init__(value)
        self.scratch.append(pltpu.SemaphoreType.DMA((1,)))

    def move(self, refs, me):
        return SumPair.move(self, (refs[0], refs[1], refs[2][:3]), me)

    def finish(self, refs, me):
        (part,), (out,), (held, send, recv, local) = refs
        mine = pltpu.make_async_copy(part.at[span(me[0] * self.n, self.n)], out, local.at[0])
        mine.start()
        mine.wait()
        self.move(refs, me).wait()
        out[...] = (out[...].astype(F32) + held[...].astype(F32)).astype(BF)


def columns(rows):
    return jnp.transpose(jnp.concatenate([rows, jnp.zeros((120, PAD), F32)], axis=0))


def row_total(gathered):
    return gathered[0:8] + gathered[8:16] + gathered[16:24] + gathered[24:32]


def back_kernel(plan, me, refs):
    ins, outs, scratch = refs
    named, sums, pairs = plan
    (gmixed_0, cot_0, resid_0, mod_0, stacked_t, cot_t, resid_t, stats_2, mod_t) = ins[:9]
    (out_0, out_1, image_seq, qkv_i, qkv_t, attn_i, attn_t, log_i, log_t) = ins[9:18]
    text_in, far = ins[18], ins[19:]
    (gresid_0, proj_0, gmixed_t, gresid_t, proj_t, image_out, dqkv_i, dqkv_t, text_out) = outs[:9]
    far_out = outs[9:]
    (own_0, own_t, stats_in, stats_all, part_t, gattn_t32, gattn_i, gattn_t) = scratch[:8]
    (text_sum, text_stack, aki, avi, akt, avt) = scratch[8:14]
    rest = list(scratch[14:])

    def take(op):
        count = len(op.scratch)
        found = rest[:count]
        del rest[:count]
        return found

    io = {
        "reduce_t": ((stacked_t,), (gmixed_t,)),
        "gather_0": ((own_0,), (proj_0,)),
        "stats": ((stats_in,), (stats_all,)),
        "gather_t": ((own_t,), (proj_t,)),
        "reduce_a": ((part_t,), (gattn_t32,)),
        "image": ((image_seq,), (image_out,)),
        "text": ((text_stack,), (text_out,)),
    }
    refs_of = {key: (*io[key], take(op)) for key, op in named.items()}
    sum_refs = [((text_in,), (text_sum,), take(op)) for op in sums]
    far_refs = [((far[i],), (far_out[i],), take(op)) for i, op in enumerate(pairs)]

    def do(key, step):
        getattr(named[key], step)(refs_of[key], me)

    do("reduce_t", "start")
    for op, part in zip(sums, sum_refs):
        op.start(part, me)

    def norm_rows(i, carry):
        at = pl.ds(pl.multiple_of(i * 64, 64), 64)
        resid = resid_0[at, :]
        mean = jnp.mean(resid, axis=1, keepdims=True)
        square = jnp.mean(resid * resid, axis=1, keepdims=True)
        inverse = lax.rsqrt(square - mean * mean + EPSILON)
        normed = (resid - mean) * inverse
        grad = gmixed_0[at, :] * (1.0 + mod_0[4:5])
        total = jnp.mean(grad, axis=1, keepdims=True)
        cross = jnp.mean(grad * normed, axis=1, keepdims=True)
        result = cot_0[at, :].astype(F32) + inverse * (grad - total - normed * cross)
        gresid_0[at, :] = result
        own_0[at, :] = (result * mod_0[2:3]).astype(BF)
        return carry

    lax.fori_loop(0, 4, norm_rows, 0)
    do("gather_0", "start")
    do("reduce_t", "finish")

    before = columns(row_total(stats_2)) / D
    mean, square = before[:, 0:1], before[:, 1:2]
    inverse = lax.rsqrt(square - mean * mean + EPSILON)
    normed = (resid_t[...] - mean) * inverse
    grad = gmixed_t[...] * (1.0 + mod_t[4:5])
    lane = lax.broadcasted_iota(jnp.int32, (PAD, 128), 1)
    pair = jnp.where(
        lane == 0,
        jnp.sum(grad, axis=1, keepdims=True),
        jnp.where(lane == 1, jnp.sum(grad * normed, axis=1, keepdims=True), 0.0),
    )
    stats_in[...] = jnp.transpose(pair)[:8]
    do("stats", "start")
    do("stats", "finish")
    after_sums = columns(row_total(stats_all)) / D
    total, cross = after_sums[:, 0:1], after_sums[:, 1:2]
    result = cot_t[...] + inverse * (grad - total - normed * cross)
    gresid_t[...] = result
    own_t[...] = (result * mod_t[2:3]).astype(BF)
    do("gather_t", "start")
    do("image", "start")
    do("gather_t", "middle")
    do("gather_t", "finish")
    for i in range(4):
        at = pl.ds(i * PAD, PAD)
        part_t[at, :] = product_right(proj_t[at, :], out_1[...]).astype(BF)
    do("reduce_a", "start")
    do("gather_0", "middle")
    for op, part in zip(sums, sum_refs):
        op.finish(part, me)
    for op, part in zip(pairs, far_refs):
        op.start(part, me)
    text = text_sum if sums else text_in
    for r in range(4):
        text_stack[pl.ds(r * 384, 384), :] = text[:, pl.ds(r * 384, 384)]
    do("text", "start")
    do("gather_0", "finish")

    def rows_back(i, carry):
        at = span(i * 256, 256)
        gattn_i[at, :] = product_right(proj_0[at, :], out_0[...]).astype(BF)
        return carry

    lax.fori_loop(0, 4, rows_back, 0)
    do("reduce_a", "finish")
    gattn_t[...] = gattn_t32[...].astype(BF)
    attend_back_body(
        qkv_i.shape[1] // 384,
        qkv_i, qkv_t, attn_i, attn_t, gattn_i, gattn_t, log_i, log_t,
        dqkv_i, dqkv_t, aki, avi, akt, avt,
    )
    do("text", "finish")
    do("image", "finish")
    for op, part in zip(pairs, far_refs):
        op.finish(part, me)


def back(number, dps, values, text, fars):
    def shape(*dims, dtype=BF):
        return jax.ShapeDtypeStruct(dims, dtype)

    named = {
        "reduce_t": ReduceScatterRow(shape(640, 384)),
        "gather_0": AllGatherCol(shape(256, 1536), 4),
        "stats": AllGatherRow(shape(8, PAD, dtype=F32)),
        "gather_t": AllGatherCol(shape(PAD, 384)),
        "reduce_a": ReduceScatterRow(shape(640, 384)),
        "image": FromSequence(shape(256, 1536)),
        "text": AllToAllRow(shape(1536, 384)),
    }
    sums = [SumPair(text)] if dps == 2 else []
    pairs = [SumPairFar(far) for far in fars]
    ops = list(named.values()) + sums + pairs
    count = 19 + len(fars)
    out_shapes = [
        shape(256, 1536, dtype=F32),
        shape(1024, 1536),
        shape(PAD, 384, dtype=F32),
        shape(PAD, 384, dtype=F32),
        shape(640, 384),
        shape(1024, 384),
        shape(1024, 1152),
        shape(PAD, 1152),
        shape(1536, 384),
    ] + [op.outs[0] for op in pairs]

    def kernel(*refs):
        me = tuple(lax.axis_index(name) for name in ("dp", "row", "col"))
        barrier = pltpu.get_barrier_semaphore()
        peers = named["gather_0"].peers(me) + named["stats"].peers(me)
        if dps == 2:
            peers = peers + sums[0].peers(me)
        for device in peers:
            pl.semaphore_signal(barrier, 1, device_id=device, device_id_type=MESH)
        image = named["image"]
        for device, wanted in image.greets(me):
            @pl.when(wanted)
            def _():
                pl.semaphore_signal(barrier, 1, device_id=device, device_id_type=MESH)
        pl.semaphore_wait(barrier, len(peers) + 4 - (me[1] == me[2]).astype(jnp.int32))
        outs = count + len(out_shapes)
        back_kernel((named, sums, pairs), me, (refs[:count], refs[count:outs], refs[outs:]))

    vmem, hbm = pl.BlockSpec(memory_space=pltpu.VMEM), pl.BlockSpec(memory_space=pl.ANY)
    return pl.pallas_call(
        kernel,
        in_specs=[vmem] * 19 + [hbm] * len(fars),
        out_specs=[vmem] * len(out_shapes),
        out_shape=out_shapes,
        scratch_shapes=[
            pltpu.VMEM((256, 1536), BF),
            pltpu.VMEM((PAD, 384), BF),
            pltpu.VMEM((8, PAD), F32),
            pltpu.VMEM((32, PAD), F32),
            pltpu.VMEM((640, 384), BF),
            pltpu.VMEM((PAD, 384), F32),
            pltpu.VMEM((1024, 384), BF),
            pltpu.VMEM((PAD, 384), BF),
            pltpu.VMEM((384, 1536), BF),
            pltpu.VMEM((1536, 384), BF),
        ]
        + [pltpu.VMEM((n, 128), F32) for n in (IMG, IMG, PAD, PAD)]
        + [item for op in ops for item in op.scratch],
        compiler_params=pltpu.CompilerParams(
            collective_id=number, has_side_effects=True, vmem_limit_bytes=62 * 1024 * 1024
        ),
        cost_estimate=cost(130),
        name="back",
    )(*values, text, *fars)


def finish_feed_kernel(up_parts, down_parts, text, up, down):
    for k in range(4):
        at = slice(k * 384, (k + 1) * 384)
        up[0, :, at] = up_parts[at].astype(F32)
        down[0, at] = down_parts[at].astype(F32)
    for r in range(4):
        starts = [k * 1536 + r * 384 for k in range(2)]
        both = [text[start : start + 192].astype(F32) for start in starts]
        up[1, :, r * 384 : (r + 1) * 384] = jnp.transpose(jnp.concatenate(both, axis=0))
        for k in range(2):
            place = r * 384 + k * 192
            down[1, place : place + 192] = text[starts[k] + 192 : starts[k] + 384].astype(F32)


def finish_rest_kernel(dps, parts, qkv_parts, out_parts, qkv, out):
    for k in range(3):
        at = slice(k * 384, (k + 1) * 384)
        qkv[0, :, at] = parts[at].astype(F32)
    out[0] = parts[1152:1536].astype(F32)
    for target, terms in ((qkv, qkv_parts), (out, out_parts)):
        total = terms[0:384].astype(F32)
        for d in range(1, dps):
            total = total + terms[d * 384 : (d + 1) * 384].astype(F32)
        target[1] = total


def finish(kernel, name, shapes, *values):
    return pl.pallas_call(
        kernel,
        in_specs=[pl.BlockSpec(memory_space=pltpu.VMEM)] * len(values),
        out_specs=[pl.BlockSpec(memory_space=pltpu.VMEM)] * len(shapes),
        out_shape=[jax.ShapeDtypeStruct(shape, F32) for shape in shapes],
        compiler_params=pltpu.CompilerParams(vmem_limit_bytes=56 * 1024 * 1024),
        cost_estimate=cost(6),
        name=name,
    )(*values)


def pad_text(values):
    return jnp.pad(values, ((0, PAD - TXT), (0, 0)))


def shards(
    dps,
    rows,
    cols,
    image_tokens,
    text_tokens,
    condition,
    ada_w,
    ada_b,
    qkv_w,
    qkv_b,
    out_w,
    out_b,
    up_w,
    up_b,
    down_w,
    down_b,
    image_cot,
    text_cot,
):
    row = lax.axis_index("row")
    col = lax.axis_index("col")
    seqs = condition.shape[0]
    wr = image_tokens.shape[1]
    wc = condition.shape[1]
    wf = up_w.shape[2]

    first_w = Weight(jnp.concatenate([qkv_w[0].reshape(wr, 3 * wc), out_w[0]], axis=1), 1)
    first_a = first_w.gather(0)
    parity = lax.rem(lax.axis_index("dp"), 2)
    qkv_1 = qkv_w[1].reshape(wr, 3 * wc)
    share = wf // rows
    up_bias_1 = lax.dynamic_slice_in_dim(up_b[1], row * share, share).astype(F32)

    cond_value = condition.astype(F32)
    silu_low = jax.nn.silu(cond_value).astype(BF)
    modul_parts = jnp.concatenate(
        [product(silu_low, ada_w[s].reshape(wc, 6 * wr)) for s in range(2)]
    )
    modul_all = exchange(1, 7, AllGatherCol(modul_parts))[0].reshape(cols, 2, seqs, 6, wr)
    mods = jnp.sum(modul_all, axis=0) + ada_b.astype(F32)[:, None]
    bias_rows = jnp.broadcast_to(
        jnp.stack([out_b[0], down_b[0]]).astype(F32)[None], (seqs, 2, wr)
    )
    sent = jnp.concatenate([mods[0], bias_rows], axis=1).reshape(seqs * 8, wr)
    x1 = pad_text(text_tokens.astype(F32))
    cot1 = pad_text(text_cot.astype(F32))
    x0, mods_row, stats = exchange(
        2,
        30,
        ToSequence(image_tokens),
        AllGatherRow(sent),
        AllGatherRow(row_stats(x1, x1 * x1)),
    )
    mod_0 = lax.dynamic_index_in_dim(
        mods_row.reshape(rows, seqs, 8, wr), row, 1, keepdims=False
    ).transpose(1, 0, 2).reshape(8, rows * wr)
    mod_1 = lax.dynamic_index_in_dim(mods[1], col, 0, keepdims=False)
    first_b = first_w.gather(1, x0)

    x0 = x0.astype(F32)
    norm1_0, inv1_0 = norm_local(x0)
    mixed1_0 = (norm1_0 * (1.0 + mod_0[1]) + mod_0[0]).astype(BF)
    norm1_1, inv1_1 = norm_row(x1, stats)
    mixed1_1 = (norm1_1 * (1.0 + mod_1[1]) + mod_1[0]).astype(BF)
    full1_1, full1_0, cot0 = exchange(
        3,
        27,
        AllGatherCol(mixed1_1),
        AllGatherCol(mixed1_0, 4),
        ToSequence(image_cot),
    )
    cot0 = cot0.astype(F32)
    qkv_bias = jnp.stack(
        [qkv_b[:, 0], jnp.zeros_like(qkv_b[:, 0]), qkv_b[:, 1]], axis=1
    ).astype(F32).reshape(2, 3 * wc)
    first_a, first_b, qkv_t, wide_g1, branch_g0 = exchange(
        4,
        45,
        first_w.swap(0, first_a),
        first_w.swap(1, first_b),
        ReduceScatterRow(product(full1_1, qkv_1).astype(BF)),
        AllGatherRow((mod_1[5] * cot1).astype(BF)),
        AllGatherCol((mod_0[5] * cot0).astype(BF), 4),
    )
    up_0, down_0 = Weight(up_w[0], 1), Weight(down_w[0], 0)
    up_a, up_b0 = up_0.gather(0, qkv_t), up_0.gather(1, qkv_t)
    down_a, down_b0 = down_0.gather(0, qkv_t), down_0.gather(1, qkv_t)
    qkv_txt = (qkv_t + qkv_bias[1]).astype(BF)
    qkv_img, qkv_0, out_0 = input_product(full1_0, [first_a, first_b], qkv_bias[:1])
    text_w = jnp.stack([up_w[1].T.reshape(rows, 2, -1, wr), down_w[1].reshape(rows, 2, -1, wr)])
    text_w, text_own = (
        lax.dynamic_index_in_dim(text_w, half, 2, keepdims=False).transpose(1, 0, 2, 3)
        for half in (parity, 1 - parity)
    )
    text_own = lax.dynamic_index_in_dim(text_own, row, 0, False).reshape(-1, wr)
    attn_0, attn_text, log_0, log_1, up_a, text_w = exchange(
        5,
        26,
        attend(qkv_img, qkv_txt),
        up_0.swap(0, up_a),
        AllToAllRow(text_w.reshape(-1, wr)),
        name="attend",
    )
    up_b0, text_w, attn_1, branch_g1 = exchange(
        6,
        32,
        up_0.swap(1, up_b0),
        SwapBlocks(text_w, text_own),
        AllGatherRow(attn_text),
        AllGatherCol(side(wide_g1, rows), 2),
    )

    down_a, proj_1, proj_0 = exchange(
        7,
        27,
        down_0.swap(0, down_a),
        ReduceScatterCol(product(attn_1, out_w[1]).astype(BF)),
        ReduceScatterCol(product(attn_0, out_0).astype(BF), 4),
    )
    proj_0 = proj_0 + mod_0[6]
    resid_0 = x0 + mod_0[2] * proj_0
    norm2_0, inv2_0 = norm_local(resid_0)
    mixed2_0 = (norm2_0 * (1.0 + mod_0[4]) + mod_0[3]).astype(BF)
    proj_1 = proj_1 + out_b[1].astype(F32)
    resid_1 = x1 + mod_1[2] * proj_1
    def by_row(left, right):
        wide = product_left(right, left).reshape(rows, wr, left.shape[1])
        return wide.transpose(0, 2, 1)

    results = feed(
        8,
        mixed2_0,
        resid_1,
        jnp.pad(jnp.stack([mod_1[3], 1.0 + mod_1[4]]), ((0, 6), (0, 0))),
        branch_g0,
        branch_g1,
        up_b[:1].astype(F32),
        up_bias_1[None],
        down_b0,
        down_0.other(1),
        down_a,
        up_a,
        up_b0,
        text_w,
    )
    mixed2_g0, wide2_g1, stats, pre_s0, pre_s1, branch_0 = results[:6]
    up_p, down_p, text_p, branch_p1 = results[6:]
    branch_0 = branch_0 + mod_0[7]
    norm2_1, inv2_1 = norm_row(resid_1, stats)
    fars = [part.reshape(-1, wr) for part in (down_p[0], down_p[1], up_p[0], up_p[1])]
    text_p = text_p.transpose(1, 0, 2, 3).reshape(-1, rows * wr)
    parity_now = lax.rem(lax.axis_index("dp"), 2)
    if dps != 2:
        halves = [
            lax.dynamic_slice_in_dim(
                lax.psum(part, "dp"), parity_now * (part.shape[0] // 2), part.shape[0] // 2
            )
            for part in fars + [text_p]
        ]
        fars, text_p = [], halves[4]
    (
        resid_g0,
        proj_g0,
        mixed2_g1,
        resid_g1,
        proj_g1,
        image_out,
        qkv_grad_0,
        qkv_grad_t,
        text_h,
        *sums,
    ) = back(
        11,
        dps,
        [
            mixed2_g0,
            cot0.astype(BF),
            resid_0,
            mod_0,
            stack(wide2_g1.astype(BF), rows),
            cot1,
            resid_1,
            stats,
            jnp.pad(mod_1, ((0, 2), (0, 0))),
            out_0,
            out_w[1],
            (resid_0 + mod_0[5] * branch_0).astype(BF),
            qkv_img,
            qkv_txt,
            attn_0,
            attn_text,
            log_0,
            log_1,
        ],
        text_p,
        fars,
    )
    down_ha, down_hb, up_ha, up_hb = [
        reduce_row(part) for part in (sums if dps == 2 else halves[:4])
    ]
    out_g1 = product_left(attn_1, proj_g1)
    qkv_p = product_left(full1_0, qkv_grad_0).astype(BF).reshape(rows, wr, 3 * wc)
    out_p = by_row(attn_0, proj_g0).astype(BF)
    parts = [qkv_p[:, :, :wc], qkv_p[:, :, wc : 2 * wc], qkv_p[:, :, 2 * wc :], out_p]
    first_pairs = [
        sum_pair(jnp.stack([parts[i], parts[2 + i]]).reshape(2, -1, wc), dps) for i in range(2)
    ]

    def column_sums(values):
        return jnp.sum(values, axis=0, dtype=F32)

    first = (row == 0).astype(F32)
    place = (lax.iota(jnp.int32, rows) == row).astype(F32)[:, None]
    qkv_s0 = column_sums(qkv_grad_0)
    qkv_s1 = column_sums(qkv_grad_t)
    vectors = jnp.concatenate(
        [
            column_sums(branch_g0),
            column_sums(proj_g0),
            column_sums(branch_g1) * first,
            (place * column_sums(proj_g1)[None]).reshape(-1),
            pre_s0[0],
            (place * pre_s1).reshape(-1),
            qkv_s0[:wc],
            qkv_s0[2 * wc :],
            qkv_s1[:wc],
            qkv_s1[2 * wc :],
        ]
    ).reshape(-1, wc)
    pad_rows = -vectors.shape[0] % 8
    qkv_grad_1, mixed1_g0, vectors, *sums = exchange(
        16,
        51,
        AllGatherRow(qkv_grad_t),
        ReduceScatterCol(product_right(qkv_grad_0, qkv_0).astype(BF), 4),
        AllGatherRow(jnp.pad(vectors, ((0, pad_rows), (0, 0)))),
        ReduceScatterCol(branch_p1, 2),
        first_pairs[0][0],
        first_pairs[1][0],
    )
    wide_1, sums = sums[0], sums[1:]
    first_ha = reduce_row(first_pairs[0][1](sums))
    first_hb = reduce_row(first_pairs[1][1](sums[1:]))
    qkv_g1 = product_left(full1_1, qkv_grad_1)
    image_grad = resid_g0 + norm_local_back(mixed1_g0 * (1.0 + mod_0[1]), norm1_0, inv1_0)
    branch_1, down_b0, mixed1_g1, text_b, vectors, image_grad = exchange(
        17,
        37,
        ReduceScatterRow(stack(wide_1.astype(BF), rows)),
        AllGatherDp(jnp.concatenate([down_ha, down_hb]), dps),
        ReduceScatterCol(product_right(qkv_grad_1, qkv_1).astype(BF)),
        AllGatherDp(text_h, dps),
        AllGatherDp(jnp.sum(vectors.reshape(rows, -1, wc), axis=0), dps),
        FromSequence(image_grad.astype(BF)),
    )
    vectors = jnp.sum(vectors.reshape(dps, -1, wc), axis=0).reshape(-1)
    branch_1 = branch_1 + down_b[1].astype(F32)
    text_out = (resid_1 + mod_1[5] * branch_1).astype(BF)[:TXT]
    norm1_g1 = mixed1_g1 * (1.0 + mod_1[1])

    sums_0 = jnp.stack(
        [
            jnp.sum(t, axis=0)
            for t in (
                mixed1_g0,
                mixed1_g0 * norm1_0,
                resid_g0 * proj_0,
                mixed2_g0,
                mixed2_g0 * norm2_0,
                cot0 * branch_0,
            )
        ]
    )
    sums_1 = jnp.stack(
        [
            jnp.sum(t, axis=0)
            for t in (
                mixed1_g1,
                mixed1_g1 * norm1_1,
                resid_g1 * proj_1,
                mixed2_g1,
                mixed2_g1 * norm2_1,
                cot1 * branch_1,
            )
        ]
    )
    up_b0, stats, cols_0, cols_1 = exchange(
        18,
        15,
        AllGatherDp(jnp.concatenate([up_ha, up_hb]), dps),
        AllGatherRow(row_stats(norm1_g1, norm1_g1 * norm1_1)),
        AllGatherCol(jnp.pad(sums_0, ((0, 2), (0, 0)))),
        AllGatherCol(jnp.pad(sums_1, ((0, 2), (0, 0)))),
    )
    image_grad = image_grad.astype(F32)
    text_grad = resid_g1 + norm_row_back(norm1_g1, norm1_1, inv1_1, stats)
    qkv_b1, rows_0 = exchange(
        19,
        19,
        AllGatherDp(qkv_g1.astype(BF), dps),
        AllGatherRow(jnp.sum(cols_0.reshape(cols, 8, rows * wr), axis=0)),
    )
    rows_0 = lax.dynamic_index_in_dim(
        rows_0.reshape(seqs, 8, rows, wr)[:, :6], row, 2, keepdims=False
    )
    mods_low = jnp.stack([rows_0, cols_1.reshape(seqs, 8, wr)[:, :6]]).astype(BF)
    mods_low = mods_low.reshape(2, seqs, 6 * wr)
    silu_part = product_right(mods_low[0], ada_w[0].reshape(wc, 6 * wr)) + product_right(
        mods_low[1], ada_w[1].reshape(wc, 6 * wr)
    )
    firsts, out_b1, mods_all, silu_all, silu_part = exchange(
        20,
        20,
        AllGatherDp(jnp.concatenate([first_ha, first_hb]), dps),
        AllGatherDp(out_g1.astype(BF), dps),
        AllGatherDp(mods_low.reshape(2 * seqs, 6 * wr).astype(F32), dps),
        AllGatherDp(jnp.pad(silu_low.astype(F32), ((0, 8 - seqs), (0, 0))), dps),
        AllGatherRow(jnp.pad(silu_part, ((0, 8 - seqs), (0, 0)))),
    )
    mods_all = mods_all.reshape(dps, 2, seqs, 6 * wr).transpose(1, 0, 2, 3)
    mods_all = mods_all.reshape(2, dps * seqs, 6 * wr).astype(BF)
    silu_all = silu_all.reshape(dps, 8, wc)[:, :seqs].reshape(dps * seqs, wc).astype(BF)
    ada_gw = jnp.stack(
        [product_left(silu_all, mods_all[s]).reshape(wc, 6, wr) for s in range(2)]
    )
    ada_gb = jnp.sum(mods_all, axis=1, dtype=F32).reshape(2, 6, wr)
    silu_sum = jnp.sum(silu_part.reshape(rows, 8, wc), axis=0)[:seqs]
    condition_grad = silu_slope(cond_value, silu_sum)
    row_sums = lax.dynamic_index_in_dim(
        vectors[: 4 * rows * wr].reshape(2, 2, rows, wr), row, 2, keepdims=False
    )
    rest = vectors[4 * rows * wr : 4 * rows * wr + 2 * wf + 4 * wc]
    up_gb = rest[: 2 * wf].reshape(2, wf)
    qkv_gb = rest[2 * wf :].reshape(2, 2, wc)

    up_g, down_g = finish(
        finish_feed_kernel, "finish_feed", [(2, wr, wf), (2, wf, wr)], up_b0, down_b0, text_b
    )
    qkv_g, out_g = finish(
        functools.partial(finish_rest_kernel, dps),
        "finish_rest",
        [(2, wr, 3 * wc), (2, wc, wr)],
        firsts,
        qkv_b1,
        out_b1,
    )

    return (
        image_out,
        text_out,
        image_grad,
        text_grad[:TXT],
        condition_grad,
        ada_gw,
        ada_gb,
        qkv_g.reshape(2, wr, 3, wc),
        qkv_gb,
        out_g,
        row_sums[:, 1],
        up_g,
        up_gb,
        down_g,
        row_sums[:, 0],
    )


def solution(mesh):
    placed = (
        P(("dp", "col"), "row"),
        P(("dp", "col"), "row"),
        P("dp", "col"),
        P(None, "col", None, "row"),
        P(None, None, "row"),
        P(None, "row", None, "col"),
        P(None, None, "col"),
        P(None, "col", "row"),
        P(None, "row"),
        P(None, "row", "col"),
        P(None, "col"),
        P(None, "col", "row"),
        P(None, "row"),
        P(("dp", "col"), "row"),
        P(("dp", "col"), "row"),
    )
    sizes = [mesh.shape[name] for name in ("dp", "row", "col")]
    return jax.shard_map(
        functools.partial(shards, *sizes),
        mesh=mesh,
        in_specs=placed,
        out_specs=(
            P(("dp", "col"), "row"),
            P(("dp", "col"), "row"),
            P(("dp", "col"), "row"),
            P(("dp", "col"), "row"),
            P("dp", "col"),
            P(None, "col", None, "row"),
            P(None, None, "row"),
            P(None, "row", None, "col"),
            P(None, None, "col"),
            P(None, "col", "row"),
            P(None, "row"),
            P(None, "row", "col"),
            P(None, "col"),
            P(None, "col", "row"),
            P(None, "row"),
        ),
        check_vma=False,
    )
```
